128 devices in a mesh: wide: 16 (over y_hi, z, core), narrow: 8 (over x, y_lo).
Axes of the slice: x: 4, y: 4 (y_hi: 2, y_lo: 2; y = y_hi * 2 + y_lo), z: 4, core: 2. Of those that a mesh axis runs over, the one named last changes fastest.
Arguments:
- field: float32 [2, 25, 4, 16384], P(None, None, None, ('wide', 'narrow')), may hold values from -6 to 6
- phase_table: float32 [2, 25, 25, 512], replicated, may hold values from -1 to 1, as said below
- phase_ids: int32 [7, 2, 8, 2048], P(None, None, 'narrow'), may hold values from 0 to 511
Outputs:
- transformed: float32 [2, 25, 4, 16384], P(None, None, None, ('wide', 'narrow'))
The draws below stay inside these ranges and needn't reach their ends.
Inputs may be any that keep to these rules, and one draw needn't show every extreme that they name: `phase_table`: real and imaginary parts of each entry are the cosine and sine of one angle.
All inputs are finite; a program needn't handle non-finite values.
Results may differ from the reference program's by a relative error of at most 0.0001.
Values sent between devices are 32-bit elements; how exact they have to be, the bound alone decides.
No kernel may reach another device: no remote copies, remote signals or barrier semaphores. Data moves between devices by JAX's collectives and lax.ppermute only.
A program may use at most 192 MiB of HBM per device.

```python
import math
import jax
import jax.numpy as jnp
import numpy as np
from jax import lax

RANK = 5
GATHERS = 4
TBOX = 128
NTAB = 512
LEVELS = 7
BOXES = 16384
N_WIDE = 16
N_NARROW = 8


def draw_phase_table(key, part):
    key = jax.random.fold_in(key, 11)
    phases = jax.random.uniform(key, (RANK * RANK, RANK * RANK, NTAB), jnp.float32, -math.pi, math.pi)
    return jnp.stack([jnp.cos(phases), jnp.sin(phases)], 0)


def plant(values, stream_key, low, high):
    dims = values.shape
    spot = [jax.random.randint(jax.random.fold_in(stream_key, axis), (), 0, dims[axis]) for axis in range(len(dims))]
    values = values.at[tuple(spot)].set(low)
    longest = dims.index(max(dims))
    spot[longest] = (spot[longest] + 1) % dims[longest]
    return values.at[tuple(spot)].set(high)


def block_levels(stream_key, extent, cuts, least, top_value):
    gain = 1.0
    for axis_at, parts in cuts:
        draws = jax.random.uniform(jax.random.fold_in(jax.random.fold_in(stream_key, 6), axis_at), (parts,), jnp.float32, least / len(cuts), top_value / len(cuts))
        gain = gain * jnp.repeat(jnp.exp(draws), extent[axis_at] // parts).reshape((-1,) + (1,) * (len(extent) - 1 - axis_at))
    return gain


def normal_values(key, dims, spread, bound, cuts=(), kind=jnp.bfloat16):
    entries = jax.random.normal(key, dims, jnp.float32) * spread
    if len(cuts) > 0:
        entries = block_levels(key, dims, cuts, -0.22, 0.18) * entries
    return jnp.clip(entries, min=-bound, max=bound).astype(kind)


def setup_inputs(seed: int = 0) -> dict:
    key_of = jax.random.split(jax.random.key(seed), 4)
    return {
        "field": normal_values(key_of[0], (2, RANK * RANK, GATHERS, BOXES), 1.0, 6.0, ((3, 128),), jnp.float32),
        "phase_table": draw_phase_table(jax.random.fold_in(key_of[3], 71), 0),
        "phase_ids": plant(jax.random.randint(key_of[2], (LEVELS, 2, N_NARROW, N_WIDE * TBOX), 0, NTAB), jax.random.fold_in(key_of[2], 1), 0, NTAB - 1).astype(jnp.int32),
    }


def level_maps(order_count):
    cheb_nodes = 0.5 + 0.5 * np.cos(np.pi * (2 * np.arange(order_count) + 1) / (2 * order_count))
    identity = np.eye(order_count)
    result = np.zeros((2, 2, order_count * order_count, order_count * order_count))
    for child_half in range(2):
        points = (cheb_nodes + child_half) / 2.0
        lagrange = np.ones((order_count, order_count))
        for column in range(order_count):
            for other_node in range(order_count):
                if other_node != column:
                    lagrange[:, column] *= (points - cheb_nodes[other_node]) / (cheb_nodes[column] - cheb_nodes[other_node])
        weight_scale = 1.0 / np.sqrt(2.0 * np.mean(np.sum(lagrange * lagrange, axis=1)))
        result[0, child_half] = weight_scale * np.kron(lagrange, identity)
        result[1, child_half] = weight_scale * np.kron(identity, lagrange)
    return result

def side_term(kept_map, phase_table, row_ids, coeffs):
    factor = jnp.take(phase_table, row_ids, axis=3)
    real_kern = (factor[0] * kept_map[:, :, None])[:, :, None, :]
    imag_kern = (factor[1] * kept_map[:, :, None])[:, :, None, :]
    real_coef = coeffs[0][None]
    imag_coef = coeffs[1][None]
    real_part = lax.optimization_barrier(jnp.sum(real_kern * real_coef - imag_kern * imag_coef, axis=1))
    imag_part = lax.optimization_barrier(jnp.sum(real_kern * imag_coef + imag_kern * real_coef, axis=1))
    return jnp.stack([real_part, imag_part])

def pair_term(maps_level, phase_table, low_coeffs, high_coeffs, low_ids, high_ids, kept_child):
    kept_map = jnp.take(maps_level, kept_child, axis=0)
    return side_term(kept_map, phase_table, low_ids, low_coeffs) + side_term(kept_map, phase_table, high_ids, high_coeffs)

def reference(field, phase_table, phase_ids):
    devices = N_WIDE * N_NARROW
    interp_maps = jnp.asarray(level_maps(RANK), jnp.float32)
    field_state = field.reshape(2, RANK * RANK, GATHERS, devices, TBOX).transpose(3, 0, 1, 2, 4)
    row_ids = phase_ids.reshape(LEVELS, 2, N_NARROW, N_WIDE, TBOX).transpose(0, 1, 3, 2, 4).reshape(LEVELS, 2, devices, TBOX)
    for level_index in range(LEVELS):
        stride = 2 ** level_index
        paired = field_state.reshape(devices // (2 * stride), 2, stride, 2, RANK * RANK, GATHERS, TBOX)
        lower_side = jnp.broadcast_to(paired[:, 0:1], paired.shape).reshape(field_state.shape)
        upper_side = jnp.broadcast_to(paired[:, 1:2], paired.shape).reshape(field_state.shape)
        kept_child = jnp.arange(devices, dtype=jnp.int32) // stride % 2
        maps_level = interp_maps[level_index % 2]

        def one_device(device_items):
            low_coeffs, high_coeffs, low_ids, high_ids, kept = device_items
            return pair_term(maps_level, phase_table, low_coeffs, high_coeffs, low_ids, high_ids, kept)
        field_state = lax.map(one_device, (lower_side, upper_side, row_ids[level_index, 0], row_ids[level_index, 1], kept_child))
    return field_state.transpose(1, 2, 3, 0, 4).reshape(2, RANK * RANK, GATHERS, devices * TBOX)
```

```python
import functools

import jax
import jax.numpy as jnp
import numpy as np
from jax import lax
from jax.experimental import pallas as pl
from jax.experimental.pallas import tpu as pltpu
from jax.sharding import PartitionSpec as P

RANK = 5
POINTS = RANK * RANK
GATHERS = 4
SLOTS = 128
NTAB = 512
BLOCK = 32
ROWS = 2 * RANK * BLOCK

VMEM = pl.BlockSpec(memory_space=pltpu.VMEM)
PARAMS = pltpu.CompilerParams(vmem_limit_bytes=40 * 1024 * 1024)


def swapped(block, axis, apart):
    count = lax.axis_size(axis)
    return lax.ppermute(block, axis, [(low, low ^ 1 << apart) for low in range(count)])


def half_weights(order_count):
    cheb_nodes = 0.5 + 0.5 * np.cos(np.pi * (2 * np.arange(order_count) + 1) / (2 * order_count))
    result = np.zeros((2, order_count, order_count))
    for child_half in range(2):
        points = (cheb_nodes + child_half) / 2.0
        lagrange = np.ones((order_count, order_count))
        for column in range(order_count):
            for other_node in range(order_count):
                if other_node != column:
                    lagrange[:, column] *= (points - cheb_nodes[other_node]) / (
                        cheb_nodes[column] - cheb_nodes[other_node]
                    )
        result[child_half] = lagrange / np.sqrt(2.0 * np.mean(np.sum(lagrange * lagrange, axis=1)))
    return result


def weight_tiles():
    tiles = np.zeros((2, BLOCK, SLOTS), np.float32)
    tiles[:, :POINTS] = half_weights(RANK).reshape(2, POINTS, 1)
    return tiles


def point(parity, shared, moving):
    return moving * RANK + shared if parity == 0 else shared * RANK + moving


def level_bit(level):
    bits = lax.axis_size("narrow").bit_length() - 1
    if level < bits:
        return lax.axis_index("narrow") // 2**level % 2
    return lax.axis_index("wide") // 2 ** (level - bits) % 2


def turned(tile):
    return jnp.concatenate([-tile[GATHERS:], tile[:GATHERS]], axis=0)


def apply_side(parity, kern, source, start, finish):
    for shared in range(RANK):
        tiles = [source(point(parity, shared, v)) for v in range(RANK)]
        turns = [turned(t) for t in tiles]
        for u in range(RANK):
            total = start(point(parity, shared, u))
            for v in range(RANK):
                row = shared * BLOCK + u * RANK + v
                real = kern(row)
                imag = kern(RANK * BLOCK + row)
                term = real * tiles[v] + imag * turns[v]
                total = term if total is None else total + term
            finish(point(parity, shared, u), total)


def gathered(ids_ref, weights_ref, hi, lo, level):
    bit = level_bit(level)
    first = ids_ref[level, 0]
    second = ids_ref[level, 1]
    own = jnp.where(bit == 0, first, second)
    partner = jnp.where(bit == 0, second, first)
    entry = lax.broadcasted_iota(jnp.int32, (NTAB, SLOTS), 0)
    hot = jnp.concatenate(
        [jnp.where(entry == own, 1.0, 0.0), jnp.where(entry == partner, 1.0, 0.0)], axis=1
    ).astype(jnp.bfloat16)
    values = jnp.dot(hi, hot, preferred_element_type=jnp.float32) + jnp.dot(
        lo, hot, preferred_element_type=jnp.float32
    )
    weights = jnp.where(bit == 0, weights_ref[0], weights_ref[1])
    weights = jnp.concatenate([weights] * (2 * RANK), axis=0)
    return values[:, :SLOTS] * weights, values[:, SLOTS:] * weights


def row_of(ref, lead=()):
    return lambda row: ref[lead + (pl.ds(row, 1), slice(None))]


def field_tile(ref):
    return lambda p: jnp.concatenate([ref[0, p], ref[1, p]], axis=0)


def state_tile(ref):
    return lambda p: ref[p]


def putter(ref):
    def put(p, tile):
        ref[p] = tile

    return put


def first_kernel(field_ref, table_ref, ids_ref, weights_ref, hi_ref, lo_ref, kern_ref, acc_ref, flat, own):
    for parity in range(2):
        flat[...] = jnp.zeros_like(flat)
        for c in range(2):
            for shared in range(RANK):
                for u in range(RANK):
                    at = (c * RANK + shared) * BLOCK + u * RANK
                    if parity == 0:
                        for v in range(RANK):
                            flat[at + v] = table_ref[c, point(0, shared, u), point(0, shared, v)]
                    else:
                        flat[pl.ds(at, RANK)] = table_ref[c, point(1, shared, u), pl.ds(shared * RANK, RANK)]
        whole = flat[...]
        hi = whole.astype(jnp.bfloat16)
        hi_ref[parity] = hi
        lo_ref[parity] = (whole - hi.astype(jnp.float32)).astype(jnp.bfloat16)
    own[...], kern_ref[...] = gathered(ids_ref, weights_ref, hi_ref[0], lo_ref[0], 0)
    apply_side(0, row_of(own), field_tile(field_ref), lambda p: None, putter(acc_ref))


def later_kernels(levels, ids_ref, weights_ref, hi_ref, lo_ref, kern_ref):
    for at, level in enumerate(levels):
        own, partner = gathered(ids_ref, weights_ref, hi_ref[level % 2], lo_ref[level % 2], level)
        kern_ref[at, 0] = own
        kern_ref[at, 1] = partner


def own_kernel(parity, at, state_ref, kern_ref, acc_ref):
    apply_side(parity, row_of(kern_ref, (at, 0)), state_tile(state_ref), lambda p: None, putter(acc_ref))


def join_first(acc_ref, kern_ref, field_ref, out_ref):
    apply_side(0, row_of(kern_ref), field_tile(field_ref), state_tile(acc_ref), putter(out_ref))


def join_kernel(parity, at, acc_ref, kern_ref, state_ref, out_ref):
    apply_side(parity, row_of(kern_ref, (at, 1)), state_tile(state_ref), state_tile(acc_ref), putter(out_ref))


def join_last(parity, at, acc_ref, kern_ref, state_ref, out_ref):
    def put(p, tile):
        out_ref[0, p] = tile[:GATHERS]
        out_ref[1, p] = tile[GATHERS:]

    apply_side(parity, row_of(kern_ref, (at, 1)), state_tile(state_ref), state_tile(acc_ref), put)


def call(kernel, outs, *args, scratch=()):
    return pl.pallas_call(
        kernel,
        out_shape=outs,
        in_specs=[VMEM] * len(args),
        out_specs=jax.tree.map(lambda _: VMEM, outs),
        scratch_shapes=scratch,
        compiler_params=PARAMS,
        cost_estimate=pl.CostEstimate(flops=2_000_000, bytes_accessed=1_000_000, transcendentals=0),
    )(*args)


def per_device(field, phase_table, phase_ids):
    narrow_bits = lax.axis_size("narrow").bit_length() - 1
    level_count = phase_ids.shape[0]
    ids = lax.dynamic_slice_in_dim(phase_ids, lax.axis_index("wide") * SLOTS, SLOTS, axis=3)
    weights = jnp.asarray(weight_tiles())
    f32 = jnp.float32
    state_shape = jax.ShapeDtypeStruct((POINTS, 2 * GATHERS, SLOTS), f32)
    table_shape = jax.ShapeDtypeStruct((2, ROWS, NTAB), jnp.bfloat16)

    def partner_of(state, level):
        if level < narrow_bits:
            return swapped(state, "narrow", level)
        return swapped(state, "wide", level - narrow_bits)

    partner = partner_of(field, 0)
    hi, lo, kern, acc = call(
        first_kernel,
        (table_shape, table_shape, jax.ShapeDtypeStruct((ROWS, SLOTS), f32), state_shape),
        field,
        phase_table,
        ids,
        weights,
        scratch=[pltpu.VMEM((ROWS, NTAB), f32), pltpu.VMEM((ROWS, SLOTS), f32)],
    )
    state = call(join_first, state_shape, acc, kern, partner)
    levels = tuple(range(1, level_count))
    kerns = call(
        functools.partial(later_kernels, levels),
        jax.ShapeDtypeStruct((len(levels), 2, ROWS, SLOTS), f32),
        ids,
        weights,
        hi,
        lo,
    )
    for level in levels:
        partner = partner_of(state, level)
        at = level - 1
        acc = call(functools.partial(own_kernel, level % 2, at), state_shape, state, kerns)
        if level < level_count - 1:
            state = call(functools.partial(join_kernel, level % 2, at), state_shape, acc, kerns, partner)
        else:
            state = call(
                functools.partial(join_last, level % 2, at),
                jax.ShapeDtypeStruct(field.shape, f32),
                acc,
                kerns,
                partner,
            )
    return state


def solution(mesh):
    in_specs = (P(None, None, None, ("wide", "narrow")), P(), P(None, None, "narrow", None))
    out_specs = P(None, None, None, ("wide", "narrow"))
    return jax.shard_map(
        per_device, mesh=mesh, in_specs=in_specs, out_specs=out_specs, check_vma=False
    )
```

```python
import functools

import jax
import jax.numpy as jnp
import numpy as np
from jax import lax
from jax.experimental import pallas as pl
from jax.experimental.pallas import tpu as pltpu
from jax.sharding import PartitionSpec as P

RANK = 5
POINTS = RANK * RANK
GATHERS = 4
SLOTS = 128
NTAB = 512
BLOCK = 64
ROWS = RANK * BLOCK

VMEM = pl.BlockSpec(memory_space=pltpu.VMEM)
PARAMS = pltpu.CompilerParams(vmem_limit_bytes=40 * 1024 * 1024)


def swapped(block, axis, bits):
    flip = sum(1 << bit for bit in bits)
    return lax.ppermute(block, axis, [(low, low ^ flip) for low in range(lax.axis_size(axis))])


def half_weights(order_count):
    cheb_nodes = 0.5 + 0.5 * np.cos(np.pi * (2 * np.arange(order_count) + 1) / (2 * order_count))
    result = np.zeros((2, order_count, order_count))
    for child_half in range(2):
        points = (cheb_nodes + child_half) / 2.0
        lagrange = np.ones((order_count, order_count))
        for column in range(order_count):
            for other_node in range(order_count):
                if other_node != column:
                    lagrange[:, column] *= (points - cheb_nodes[other_node]) / (
                        cheb_nodes[column] - cheb_nodes[other_node]
                    )
        result[child_half] = lagrange / np.sqrt(2.0 * np.mean(np.sum(lagrange * lagrange, axis=1)))
    return result


def weight_tiles():
    tiles = np.zeros((2, BLOCK, SLOTS), np.float32)
    tiles[:, : 2 * POINTS] = np.repeat(half_weights(RANK).reshape(2, POINTS, 1), 2, axis=1)
    return tiles


def point(parity, shared, moving):
    return moving * RANK + shared if parity == 0 else shared * RANK + moving


def level_bit(level):
    bits = lax.axis_size("narrow").bit_length() - 1
    if level < bits:
        return lax.axis_index("narrow") // 2**level % 2
    return lax.axis_index("wide") // 2 ** (level - bits) % 2


def turned(tile):
    return jnp.concatenate([-tile[GATHERS:], tile[:GATHERS]], axis=0)


def apply_side(parity, kern, source, start, finish):
    for shared in range(RANK):
        tiles = [source(point(parity, shared, v)) for v in range(RANK)]
        turns = [turned(t) for t in tiles]
        for u in range(RANK):
            total = start(point(parity, shared, u))
            for v in range(RANK):
                row = shared * BLOCK + 2 * (u * RANK + v)
                real = kern(row)
                imag = kern(row + 1)
                term = real * tiles[v] + imag * turns[v]
                total = term if total is None else total + term
            finish(point(parity, shared, u), total)


def gathered(first, second, bit, weights_ref, hi, lo):
    own = jnp.where(bit == 0, first, second)
    partner = jnp.where(bit == 0, second, first)
    entry = lax.broadcasted_iota(jnp.int32, (NTAB, SLOTS), 0)
    hot = jnp.concatenate(
        [jnp.where(entry == own, 1.0, 0.0), jnp.where(entry == partner, 1.0, 0.0)], axis=1
    ).astype(jnp.bfloat16)
    values = jnp.dot(hi, hot, preferred_element_type=jnp.float32) + jnp.dot(
        lo, hot, preferred_element_type=jnp.float32
    )
    weights = jnp.where(bit == 0, weights_ref[0], weights_ref[1])
    weights = jnp.concatenate([weights] * RANK, axis=0)
    return values[:, :SLOTS] * weights, values[:, SLOTS:] * weights


def kern_rows(ref, *lead):
    return lambda row: ref[lead + (pl.ds(row, 1), slice(None))]


def tiles_of(ref):
    if ref.shape[1] == POINTS:
        return lambda p: jnp.concatenate([ref[0, p], ref[1, p]], axis=0)
    return lambda p: ref[p]


def nothing(p):
    return None


def putter(ref):
    def put(p, tile):
        if ref.shape[1] == POINTS:
            ref[0, p] = tile[:GATHERS]
            ref[1, p] = tile[GATHERS:]
        else:
            ref[p] = tile

    return put


def first_kernel(field_ref, table_ref, ids_ref, weights_ref, hi_ref, lo_ref, kern_ref, acc_ref, flat, own):
    for parity in range(2):
        for shared in range(RANK):
            for u in range(RANK):
                for v in range(RANK):
                    at = shared * BLOCK + 2 * (u * RANK + v)
                    flat[pl.ds(at, 2)] = table_ref[point(parity, shared, u), point(parity, shared, v)]
            tail = shared * BLOCK + 2 * POINTS
            flat[pl.ds(tail, BLOCK - 2 * POINTS)] = jnp.zeros((BLOCK - 2 * POINTS, NTAB), jnp.float32)
        whole = flat[...]
        hi = whole.astype(jnp.bfloat16)
        hi_ref[parity] = hi
        lo_ref[parity] = (whole - hi.astype(jnp.float32)).astype(jnp.bfloat16)
    own[...], kern_ref[...] = gathered(
        ids_ref[0, 0], ids_ref[0, 1], level_bit(0), weights_ref, hi_ref[0], lo_ref[0]
    )
    apply_side(0, kern_rows(own), tiles_of(field_ref), nothing, putter(acc_ref))


def later_kernels(pairs, ids_ref, other_ref, weights_ref, hi_ref, lo_ref, kern_ref):
    for at, (level, mine) in enumerate(pairs):
        ids = ids_ref if mine else other_ref
        parity = level % 2
        kern_ref[at, 0], kern_ref[at, 1] = gathered(
            ids[level, 0], ids[level, 1], level_bit(level), weights_ref, hi_ref[parity], lo_ref[parity]
        )


def join_first(acc_ref, kern_ref, field_ref, ids_ref, out_ref):
    apply_side(0, kern_rows(kern_ref), tiles_of(field_ref), tiles_of(acc_ref), putter(out_ref))
    out_ref[POINTS] = jnp.concatenate(
        [ids_ref[1, s].astype(jnp.float32) for s in range(2)] + [jnp.zeros((6, SLOTS), jnp.float32)], axis=0
    )


def half_kernel(parity, at, side, state_ref, kern_ref, acc_ref):
    apply_side(parity, kern_rows(kern_ref, at, side), tiles_of(state_ref), nothing, putter(acc_ref))


def join_kernel(parity, at, acc_ref, kern_ref, state_ref, out_ref):
    apply_side(parity, kern_rows(kern_ref, at, 1), tiles_of(state_ref), tiles_of(acc_ref), putter(out_ref))


def other_first(level, state_ref, weights_ref, hi_ref, lo_ref, kern_ref, acc_ref, own):
    parity = level % 2
    ids = state_ref[POINTS].astype(jnp.int32)
    own[...], kern_ref[...] = gathered(
        ids[0:1], ids[1:2], level_bit(level), weights_ref, hi_ref[parity], lo_ref[parity]
    )
    apply_side(parity, kern_rows(own), tiles_of(state_ref), nothing, putter(acc_ref))


def far_kernel(parity, kern_at, at, acc_ref, kern_ref, state_ref, kerns_ref, out_ref, mid):
    apply_side(parity, kern_rows(kern_ref, *kern_at), tiles_of(state_ref), tiles_of(acc_ref), putter(mid))
    apply_side(1 - parity, kern_rows(kerns_ref, at, 1), tiles_of(mid), nothing, putter(out_ref))


def near_kernel(parity, at, later, acc_ref, far_ref, kerns_ref, state_ref, out_ref, mid):
    apply_side(parity, kern_rows(kerns_ref, at, 1), tiles_of(state_ref), tiles_of(acc_ref), putter(mid))
    apply_side(1 - parity, kern_rows(kerns_ref, later, 0), tiles_of(mid), tiles_of(far_ref), putter(out_ref))


def call(kernel, outs, *args, scratch=()):
    return pl.pallas_call(
        kernel,
        out_shape=outs,
        in_specs=[VMEM] * len(args),
        out_specs=jax.tree.map(lambda _: VMEM, outs),
        scratch_shapes=scratch,
        compiler_params=PARAMS,
        cost_estimate=pl.CostEstimate(flops=2_000_000, bytes_accessed=1_000_000, transcendentals=0),
    )(*args)


def per_device(field, phase_table, phase_ids):
    narrow_bits = lax.axis_size("narrow").bit_length() - 1
    wide_index = lax.axis_index("wide")
    other_index = wide_index ^ 1 << 5 - narrow_bits
    ids = lax.dynamic_slice_in_dim(phase_ids, wide_index * SLOTS, SLOTS, axis=3)
    other_ids = lax.dynamic_slice_in_dim(phase_ids, other_index * SLOTS, SLOTS, axis=3)
    table = phase_table.transpose(1, 2, 0, 3)
    weights = jnp.asarray(weight_tiles())
    f32 = jnp.float32
    state_shape = jax.ShapeDtypeStruct((POINTS, 2 * GATHERS, SLOTS), f32)
    tagged_shape = jax.ShapeDtypeStruct((POINTS + 1, 2 * GATHERS, SLOTS), f32)
    table_shape = jax.ShapeDtypeStruct((2, ROWS, NTAB), jnp.bfloat16)
    kern_shape = jax.ShapeDtypeStruct((ROWS, SLOTS), f32)
    state_scratch = pltpu.VMEM(state_shape.shape, f32)
    kern_scratch = pltpu.VMEM(kern_shape.shape, f32)
    bind = functools.partial

    def partner_of(state, *levels):
        if levels[0] < narrow_bits:
            return swapped(state, "narrow", list(levels))
        return swapped(state, "wide", [level - narrow_bits for level in levels])

    partner = partner_of(field, 0)
    hi, lo, kern, acc = call(
        first_kernel,
        (table_shape, table_shape, kern_shape, state_shape),
        field,
        table,
        ids,
        weights,
        scratch=[pltpu.VMEM((ROWS, NTAB), f32), kern_scratch],
    )
    state = call(join_first, tagged_shape, acc, kern, partner, ids)

    near, both, far = partner_of(state, 1), partner_of(state, 1, 2), partner_of(state, 2)
    pairs = ((1, True), (2, True), (3, True), (4, True), (4, False), (5, True), (6, True))
    kerns = call(
        bind(later_kernels, pairs),
        jax.ShapeDtypeStruct((len(pairs), 2, ROWS, SLOTS), f32),
        ids,
        other_ids,
        weights,
        hi,
        lo,
    )
    acc = call(bind(half_kernel, 1, 0, 0), state_shape, state, kerns)
    kern, other = call(
        bind(other_first, 1), (kern_shape, state_shape), far, weights, hi, lo, scratch=[kern_scratch]
    )
    other = call(bind(far_kernel, 1, (), 1), state_shape, other, kern, both, kerns, scratch=[state_scratch])
    state = call(bind(near_kernel, 1, 0, 1), state_shape, acc, other, kerns, near, scratch=[state_scratch])

    partner = partner_of(state, 3)
    acc = call(bind(half_kernel, 1, 2, 0), state_shape, state, kerns)
    state = call(bind(join_kernel, 1, 2), state_shape, acc, kerns, partner)

    near, both, far = partner_of(state, 4), partner_of(state, 4, 5), partner_of(state, 5)
    acc = call(bind(half_kernel, 0, 3, 0), state_shape, state, kerns)
    other = call(bind(half_kernel, 0, 4, 0), state_shape, far, kerns)
    other = call(bind(far_kernel, 0, (4, 1), 5), state_shape, other, kerns, both, kerns, scratch=[state_scratch])
    state = call(bind(near_kernel, 0, 3, 5), state_shape, acc, other, kerns, near, scratch=[state_scratch])

    partner = partner_of(state, 6)
    acc = call(bind(half_kernel, 0, 6, 0), state_shape, state, kerns)
    return call(bind(join_kernel, 0, 6), jax.ShapeDtypeStruct(field.shape, f32), acc, kerns, partner)


def solution(mesh):
    in_specs = (P(None, None, None, ("wide", "narrow")), P(), P(None, None, "narrow", None))
    out_specs = P(None, None, None, ("wide", "narrow"))
    return jax.shard_map(
        per_device, mesh=mesh, in_specs=in_specs, out_specs=out_specs, check_vma=False
    )
```

```python
import functools

import jax
import jax.numpy as jnp
import numpy as np
from jax import lax
from jax.experimental import pallas as pl
from jax.experimental.pallas import tpu as pltpu
from jax.sharding import PartitionSpec as P

RANK = 5
POINTS = RANK * RANK
GATHERS = 4
SLOTS = 128
NTAB = 512
BLOCK = 64
ROWS = RANK * BLOCK

VMEM = pl.BlockSpec(memory_space=pltpu.VMEM)
HBM = pl.BlockSpec(memory_space=pltpu.HBM)
MIB = 1024 * 1024


def swapped(block, axis, bits):
    flip = sum(1 << bit for bit in bits)
    return lax.ppermute(block, axis, [(low, low ^ flip) for low in range(lax.axis_size(axis))])


def half_weights(order_count):
    cheb_nodes = 0.5 + 0.5 * np.cos(np.pi * (2 * np.arange(order_count) + 1) / (2 * order_count))
    result = np.zeros((2, order_count, order_count))
    for child_half in range(2):
        points = (cheb_nodes + child_half) / 2.0
        lagrange = np.ones((order_count, order_count))
        for column in range(order_count):
            for other_node in range(order_count):
                if other_node != column:
                    lagrange[:, column] *= (points - cheb_nodes[other_node]) / (
                        cheb_nodes[column] - cheb_nodes[other_node]
                    )
        result[child_half] = lagrange / np.sqrt(2.0 * np.mean(np.sum(lagrange * lagrange, axis=1)))
    return result


def weight_tiles():
    tiles = np.zeros((2, BLOCK, SLOTS), np.float32)
    tiles[:, : 2 * POINTS] = np.repeat(half_weights(RANK).reshape(2, POINTS, 1), 2, axis=1)
    return tiles


def point(parity, shared, moving):
    return moving * RANK + shared if parity == 0 else shared * RANK + moving


def level_bit(level):
    bits = lax.axis_size("narrow").bit_length() - 1
    if level < bits:
        return lax.axis_index("narrow") // 2**level % 2
    return lax.axis_index("wide") // 2 ** (level - bits) % 2


def turned(tile):
    return jnp.concatenate([-tile[GATHERS:], tile[:GATHERS]], axis=0)


def apply_side(parity, kern, source, start, finish):
    for shared in range(RANK):
        tiles = [source(point(parity, shared, v)) for v in range(RANK)]
        turns = [turned(t) for t in tiles]
        for u in range(RANK):
            total = start(point(parity, shared, u))
            for v in range(RANK):
                row = shared * BLOCK + 2 * (u * RANK + v)
                real = kern(row)
                imag = kern(row + 1)
                term = real * tiles[v] + imag * turns[v]
                total = term if total is None else total + term
            finish(point(parity, shared, u), total)


def gathered(first, second, bit, weights_ref, hi, lo):
    own = jnp.where(bit == 0, first, second)
    partner = jnp.where(bit == 0, second, first)
    entry = lax.broadcasted_iota(jnp.int32, (NTAB, SLOTS), 0)
    hot = jnp.concatenate(
        [jnp.where(entry == own, 1.0, 0.0), jnp.where(entry == partner, 1.0, 0.0)], axis=1
    ).astype(jnp.bfloat16)
    values = jnp.dot(hi, hot, preferred_element_type=jnp.float32) + jnp.dot(
        lo, hot, preferred_element_type=jnp.float32
    )
    weights = jnp.where(bit == 0, weights_ref[0], weights_ref[1])
    weights = jnp.concatenate([weights] * RANK, axis=0)
    return values[:, :SLOTS] * weights, values[:, SLOTS:] * weights


def kern_rows(ref, *lead):
    return lambda row: ref[lead + (pl.ds(row, 1), slice(None))]


def tiles_of(ref):
    if ref.shape[1] == POINTS:
        return lambda p: jnp.concatenate([ref[0, p], ref[1, p]], axis=0)
    return lambda p: ref[p]


def nothing(p):
    return None


def putter(ref):
    def put(p, tile):
        if ref.shape[1] == POINTS:
            ref[0, p] = tile[:GATHERS]
            ref[1, p] = tile[GATHERS:]
        else:
            ref[p] = tile

    return put


def table_kernel(table_hbm, hi_ref, lo_ref, table, flat, sems):
    copies = []
    for parity in range(2):
        for shared in range(RANK):
            if parity == 0:
                source = table_hbm.at[:, shared, :, shared]
            else:
                source = table_hbm.at[shared, :, shared, :]
            copies.append(pltpu.make_async_copy(source, table.at[parity, shared], sems.at[len(copies)]))
            copies[-1].start()
    for parity in range(2):
        for shared in range(RANK):
            tail = shared * BLOCK + 2 * POINTS
            flat[pl.ds(tail, BLOCK - 2 * POINTS)] = jnp.zeros((BLOCK - 2 * POINTS, NTAB), jnp.float32)
            copies[parity * RANK + shared].wait()
            for u in range(RANK):
                for v in range(RANK):
                    flat[pl.ds(shared * BLOCK + 2 * (u * RANK + v), 2)] = table[parity, shared, u, v]
        whole = flat[...]
        hi = whole.astype(jnp.bfloat16)
        hi_ref[parity] = hi
        lo_ref[parity] = (whole - hi.astype(jnp.float32)).astype(jnp.bfloat16)


def first_kernel(
    other_flip, field_ref, all_ids_ref, weights_ref, hi_ref, lo_ref, kern_ref, acc_ref, ids_ref, other_ref, own
):
    wide_index = lax.axis_index("wide")
    for device, ref in ((wide_index, ids_ref), (wide_index ^ other_flip, other_ref)):
        ref[...] = all_ids_ref[:, :, :, pl.ds(pl.multiple_of(device * SLOTS, SLOTS), SLOTS)]
    own[...], kern_ref[...] = gathered(
        ids_ref[0, 0], ids_ref[0, 1], level_bit(0), weights_ref, hi_ref[0], lo_ref[0]
    )
    apply_side(0, kern_rows(own), tiles_of(field_ref), nothing, putter(acc_ref))


def later_kernels(pairs, ids_ref, other_ref, weights_ref, hi_ref, lo_ref, kern_ref):
    for at, (level, mine) in enumerate(pairs):
        ids = ids_ref if mine else other_ref
        parity = level % 2
        kern_ref[at, 0], kern_ref[at, 1] = gathered(
            ids[level, 0], ids[level, 1], level_bit(level), weights_ref, hi_ref[parity], lo_ref[parity]
        )


def join_first(acc_ref, kern_ref, field_ref, ids_ref, out_ref):
    apply_side(0, kern_rows(kern_ref), tiles_of(field_ref), tiles_of(acc_ref), putter(out_ref))
    out_ref[POINTS] = jnp.concatenate(
        [ids_ref[1, s].astype(jnp.float32) for s in range(2)] + [jnp.zeros((6, SLOTS), jnp.float32)], axis=0
    )


def half_kernel(parity, at, side, state_ref, kern_ref, acc_ref):
    apply_side(parity, kern_rows(kern_ref, at, side), tiles_of(state_ref), nothing, putter(acc_ref))


def join_kernel(parity, at, acc_ref, kern_ref, state_ref, out_ref):
    apply_side(parity, kern_rows(kern_ref, at, 1), tiles_of(state_ref), tiles_of(acc_ref), putter(out_ref))


def other_first(level, state_ref, weights_ref, hi_ref, lo_ref, kern_ref, acc_ref, own):
    parity = level % 2
    ids = state_ref[POINTS].astype(jnp.int32)
    own[...], kern_ref[...] = gathered(
        ids[0:1], ids[1:2], level_bit(level), weights_ref, hi_ref[parity], lo_ref[parity]
    )
    apply_side(parity, kern_rows(own), tiles_of(state_ref), nothing, putter(acc_ref))


def far_kernel(parity, kern_at, at, acc_ref, kern_ref, state_ref, kerns_ref, out_ref, mid):
    apply_side(parity, kern_rows(kern_ref, *kern_at), tiles_of(state_ref), tiles_of(acc_ref), putter(mid))
    apply_side(1 - parity, kern_rows(kerns_ref, at, 1), tiles_of(mid), nothing, putter(out_ref))


def near_kernel(parity, at, later, acc_ref, far_ref, kerns_ref, state_ref, out_ref, mid):
    apply_side(parity, kern_rows(kerns_ref, at, 1), tiles_of(state_ref), tiles_of(acc_ref), putter(mid))
    apply_side(1 - parity, kern_rows(kerns_ref, later, 0), tiles_of(mid), tiles_of(far_ref), putter(out_ref))


def call(kernel, outs, *args, scratch=(), space=VMEM, limit=40 * MIB, moved=MIB):
    return pl.pallas_call(
        kernel,
        out_shape=outs,
        in_specs=[space] * len(args),
        out_specs=jax.tree.map(lambda _: VMEM, outs),
        scratch_shapes=scratch,
        compiler_params=pltpu.CompilerParams(vmem_limit_bytes=limit),
        cost_estimate=pl.CostEstimate(flops=2_000_000, bytes_accessed=moved, transcendentals=0),
    )(*args)


def per_device(field, phase_table, phase_ids):
    narrow_bits = lax.axis_size("narrow").bit_length() - 1
    level_count = phase_ids.shape[0]
    other_flip = 1 << 5 - narrow_bits
    table = phase_table.transpose(1, 2, 0, 3).reshape(RANK, RANK, RANK, RANK, 2, NTAB)
    f32 = jnp.float32
    state_shape = jax.ShapeDtypeStruct((POINTS, 2 * GATHERS, SLOTS), f32)
    tagged_shape = jax.ShapeDtypeStruct((POINTS + 1, 2 * GATHERS, SLOTS), f32)
    table_shape = jax.ShapeDtypeStruct((2, ROWS, NTAB), jnp.bfloat16)
    kern_shape = jax.ShapeDtypeStruct((ROWS, SLOTS), f32)
    state_scratch = pltpu.VMEM(state_shape.shape, f32)
    kern_scratch = pltpu.VMEM(kern_shape.shape, f32)
    bind = functools.partial

    def partner_of(state, *levels):
        if levels[0] < narrow_bits:
            return swapped(state, "narrow", list(levels))
        return swapped(state, "wide", [level - narrow_bits for level in levels])

    partner = partner_of(field, 0)
    ids_shape = jax.ShapeDtypeStruct((level_count, 2, 1, SLOTS), jnp.int32)
    weights = jnp.asarray(weight_tiles())
    hi, lo = call(
        table_kernel,
        (table_shape, table_shape),
        table,
        scratch=[
            pltpu.VMEM((2, RANK, RANK, RANK, 2, NTAB), f32),
            pltpu.VMEM((ROWS, NTAB), f32),
            pltpu.SemaphoreType.DMA((2 * RANK,)),
        ],
        space=HBM,
        limit=51 * MIB,
        moved=5 * MIB,
    )
    kern, acc, ids, other_ids = call(
        bind(first_kernel, other_flip),
        (kern_shape, state_shape, ids_shape, ids_shape),
        field,
        phase_ids,
        weights,
        hi,
        lo,
        scratch=[kern_scratch],
    )
    state = call(join_first, tagged_shape, acc, kern, partner, ids)

    near, both, far = partner_of(state, 1), partner_of(state, 1, 2), partner_of(state, 2)
    pairs = ((1, True), (2, True), (3, True), (4, True), (4, False), (5, True), (6, True))
    kerns = call(
        bind(later_kernels, pairs),
        jax.ShapeDtypeStruct((len(pairs), 2, ROWS, SLOTS), f32),
        ids,
        other_ids,
        weights,
        hi,
        lo,
    )
    acc = call(bind(half_kernel, 1, 0, 0), state_shape, state, kerns)
    kern, other = call(
        bind(other_first, 1), (kern_shape, state_shape), far, weights, hi, lo, scratch=[kern_scratch]
    )
    other = call(bind(far_kernel, 1, (), 1), state_shape, other, kern, both, kerns, scratch=[state_scratch])
    state = call(bind(near_kernel, 1, 0, 1), state_shape, acc, other, kerns, near, scratch=[state_scratch])

    partner = partner_of(state, 3)
    acc = call(bind(half_kernel, 1, 2, 0), state_shape, state, kerns)
    state = call(bind(join_kernel, 1, 2), state_shape, acc, kerns, partner)

    near, both, far = partner_of(state, 4), partner_of(state, 4, 5), partner_of(state, 5)
    acc = call(bind(half_kernel, 0, 3, 0), state_shape, state, kerns)
    other = call(bind(half_kernel, 0, 4, 0), state_shape, far, kerns)
    other = call(bind(far_kernel, 0, (4, 1), 5), state_shape, other, kerns, both, kerns, scratch=[state_scratch])
    state = call(bind(near_kernel, 0, 3, 5), state_shape, acc, other, kerns, near, scratch=[state_scratch])

    partner = partner_of(state, 6)
    acc = call(bind(half_kernel, 0, 6, 0), state_shape, state, kerns)
    return call(bind(join_kernel, 0, 6), jax.ShapeDtypeStruct(field.shape, f32), acc, kerns, partner)


def solution(mesh):
    in_specs = (P(None, None, None, ("wide", "narrow")), P(), P(None, None, "narrow", None))
    out_specs = P(None, None, None, ("wide", "narrow"))
    return jax.shard_map(
        per_device, mesh=mesh, in_specs=in_specs, out_specs=out_specs, check_vma=False
    )
```

```python
import functools

import jax
import jax.numpy as jnp
import numpy as np
from jax import lax
from jax.experimental import pallas as pl
from jax.experimental.pallas import tpu as pltpu
from jax.sharding import PartitionSpec as P

RANK = 5
POINTS = RANK * RANK
GATHERS = 4
SLOTS = 128
NTAB = 512
BLOCK = 64
ROWS = RANK * BLOCK

VMEM = pl.BlockSpec(memory_space=pltpu.VMEM)
HBM = pl.BlockSpec(memory_space=pltpu.HBM)
MIB = 1024 * 1024


def swapped(block, axis, bits):
    flip = sum(1 << bit for bit in bits)
    return lax.ppermute(block, axis, [(low, low ^ flip) for low in range(lax.axis_size(axis))])


def half_weights(order_count):
    cheb_nodes = 0.5 + 0.5 * np.cos(np.pi * (2 * np.arange(order_count) + 1) / (2 * order_count))
    result = np.zeros((2, order_count, order_count))
    for child_half in range(2):
        points = (cheb_nodes + child_half) / 2.0
        lagrange = np.ones((order_count, order_count))
        for column in range(order_count):
            for other_node in range(order_count):
                if other_node != column:
                    lagrange[:, column] *= (points - cheb_nodes[other_node]) / (
                        cheb_nodes[column] - cheb_nodes[other_node]
                    )
        result[child_half] = lagrange / np.sqrt(2.0 * np.mean(np.sum(lagrange * lagrange, axis=1)))
    return result


def weight_tiles():
    tiles = np.zeros((2, BLOCK, SLOTS), np.float32)
    tiles[:, : 2 * POINTS] = np.repeat(half_weights(RANK).reshape(2, POINTS, 1), 2, axis=1)
    return tiles


def point(parity, shared, moving):
    return moving * RANK + shared if parity == 0 else shared * RANK + moving


def level_bit(level):
    bits = lax.axis_size("narrow").bit_length() - 1
    if level < bits:
        return lax.axis_index("narrow") // 2**level % 2
    return lax.axis_index("wide") // 2 ** (level - bits) % 2


def turned(tile):
    return jnp.concatenate([-tile[GATHERS:], tile[:GATHERS]], axis=0)


def apply_side(parity, kern, source, start, finish):
    for shared in range(RANK):
        tiles = [source(point(parity, shared, v)) for v in range(RANK)]
        turns = [turned(t) for t in tiles]
        for u in range(RANK):
            total = start(point(parity, shared, u))
            for v in range(RANK):
                row = shared * BLOCK + 2 * (u * RANK + v)
                real = kern(row)
                imag = kern(row + 1)
                term = real * tiles[v] + imag * turns[v]
                total = term if total is None else total + term
            finish(point(parity, shared, u), total)


def gathered(first, second, bit, weights_ref, hi, lo):
    own = jnp.where(bit == 0, first, second)
    partner = jnp.where(bit == 0, second, first)
    entry = lax.broadcasted_iota(jnp.int32, (NTAB, SLOTS), 0)
    hot = jnp.concatenate(
        [jnp.where(entry == own, 1.0, 0.0), jnp.where(entry == partner, 1.0, 0.0)], axis=1
    ).astype(jnp.bfloat16)
    values = jnp.dot(hi, hot, preferred_element_type=jnp.float32) + jnp.dot(
        lo, hot, preferred_element_type=jnp.float32
    )
    weights = jnp.where(bit == 0, weights_ref[0], weights_ref[1])
    weights = jnp.concatenate([weights] * RANK, axis=0)
    return values[:, :SLOTS] * weights, values[:, SLOTS:] * weights


def kern_rows(ref, *lead):
    return lambda row: ref[lead + (pl.ds(row, 1), slice(None))]


def tiles_of(ref):
    if ref.shape[1] == POINTS:
        return lambda p: jnp.concatenate([ref[0, p], ref[1, p]], axis=0)
    return lambda p: ref[p]


def nothing(p):
    return None


def putter(ref):
    def put(p, tile):
        if ref.shape[1] == POINTS:
            ref[0, p] = tile[:GATHERS]
            ref[1, p] = tile[GATHERS:]
        else:
            ref[p] = tile

    return put


def table_kernel(table_hbm, hi_ref, lo_ref, table, flat, sems):
    copies = []
    for parity in range(2):
        for shared in range(RANK):
            if parity == 0:
                source = table_hbm.at[:, shared, :, shared]
            else:
                source = table_hbm.at[shared, :, shared, :]
            copies.append(pltpu.make_async_copy(source, table.at[parity, shared], sems.at[len(copies)]))
            copies[-1].start()
    for parity in range(2):
        for shared in range(RANK):
            tail = shared * BLOCK + 2 * POINTS
            flat[pl.ds(tail, BLOCK - 2 * POINTS)] = jnp.zeros((BLOCK - 2 * POINTS, NTAB), jnp.float32)
            copies[parity * RANK + shared].wait()
            for u in range(RANK):
                for v in range(RANK):
                    flat[pl.ds(shared * BLOCK + 2 * (u * RANK + v), 2)] = table[parity, shared, u, v]
        whole = flat[...]
        hi = whole.astype(jnp.bfloat16)
        hi_ref[parity] = hi
        lo_ref[parity] = (whole - hi.astype(jnp.float32)).astype(jnp.bfloat16)


def first_kernel(
    other_flip, field_ref, all_ids_ref, weights_ref, hi_ref, lo_ref, kern_ref, acc_ref, ids_ref, other_ref, own
):
    wide_index = lax.axis_index("wide")
    for device, ref in ((wide_index, ids_ref), (wide_index ^ other_flip, other_ref)):
        ref[...] = all_ids_ref[:, :, :, pl.ds(pl.multiple_of(device * SLOTS, SLOTS), SLOTS)]
    own[...], kern_ref[...] = gathered(
        ids_ref[0, 0], ids_ref[0, 1], level_bit(0), weights_ref, hi_ref[0], lo_ref[0]
    )
    apply_side(0, kern_rows(own), tiles_of(field_ref), nothing, putter(acc_ref))


def later_kernels(pairs, ids_ref, other_ref, weights_ref, hi_ref, lo_ref, kern_ref):
    for at, (level, mine) in enumerate(pairs):
        ids = ids_ref if mine else other_ref
        parity = level % 2
        kern_ref[at, 0], kern_ref[at, 1] = gathered(
            ids[level, 0], ids[level, 1], level_bit(level), weights_ref, hi_ref[parity], lo_ref[parity]
        )


def join_first(acc_ref, kern_ref, field_ref, ids_ref, out_ref):
    apply_side(0, kern_rows(kern_ref), tiles_of(field_ref), tiles_of(acc_ref), putter(out_ref))
    out_ref[POINTS] = jnp.concatenate(
        [ids_ref[1, s].astype(jnp.float32) for s in range(2)] + [jnp.zeros((6, SLOTS), jnp.float32)], axis=0
    )


def half_kernel(parity, at, side, state_ref, kern_ref, acc_ref):
    apply_side(parity, kern_rows(kern_ref, at, side), tiles_of(state_ref), nothing, putter(acc_ref))


def join_kernel(parity, at, acc_ref, kern_ref, state_ref, out_ref):
    apply_side(parity, kern_rows(kern_ref, at, 1), tiles_of(state_ref), tiles_of(acc_ref), putter(out_ref))


def other_first(level, state_ref, weights_ref, hi_ref, lo_ref, kern_ref, acc_ref, own):
    parity = level % 2
    ids = state_ref[POINTS].astype(jnp.int32)
    own[...], kern_ref[...] = gathered(
        ids[0:1], ids[1:2], level_bit(level), weights_ref, hi_ref[parity], lo_ref[parity]
    )
    apply_side(parity, kern_rows(own), tiles_of(state_ref), nothing, putter(acc_ref))


def far_kernel(parity, kern_at, at, acc_ref, kern_ref, state_ref, kerns_ref, out_ref, mid):
    apply_side(parity, kern_rows(kern_ref, *kern_at), tiles_of(state_ref), tiles_of(acc_ref), putter(mid))
    apply_side(1 - parity, kern_rows(kerns_ref, at, 1), tiles_of(mid), nothing, putter(out_ref))


def near_kernel(parity, at, later, acc_ref, far_ref, kerns_ref, later_ref, state_ref, out_ref, mid):
    apply_side(parity, kern_rows(kerns_ref, at, 1), tiles_of(state_ref), tiles_of(acc_ref), putter(mid))
    apply_side(1 - parity, kern_rows(later_ref, later, 0), tiles_of(mid), tiles_of(far_ref), putter(out_ref))


def call(kernel, outs, *args, scratch=(), space=VMEM, limit=40 * MIB, moved=MIB):
    return pl.pallas_call(
        kernel,
        out_shape=outs,
        in_specs=[space] * len(args),
        out_specs=jax.tree.map(lambda _: VMEM, outs),
        scratch_shapes=scratch,
        compiler_params=pltpu.CompilerParams(vmem_limit_bytes=limit),
        cost_estimate=pl.CostEstimate(flops=2_000_000, bytes_accessed=moved, transcendentals=0),
    )(*args)


def per_device(field, phase_table, phase_ids):
    narrow_bits = lax.axis_size("narrow").bit_length() - 1
    level_count = phase_ids.shape[0]
    other_flip = 1 << 5 - narrow_bits
    table = phase_table.transpose(1, 2, 0, 3).reshape(RANK, RANK, RANK, RANK, 2, NTAB)
    f32 = jnp.float32
    state_shape = jax.ShapeDtypeStruct((POINTS, 2 * GATHERS, SLOTS), f32)
    tagged_shape = jax.ShapeDtypeStruct((POINTS + 1, 2 * GATHERS, SLOTS), f32)
    table_shape = jax.ShapeDtypeStruct((2, ROWS, NTAB), jnp.bfloat16)
    kern_shape = jax.ShapeDtypeStruct((ROWS, SLOTS), f32)
    state_scratch = pltpu.VMEM(state_shape.shape, f32)
    kern_scratch = pltpu.VMEM(kern_shape.shape, f32)
    bind = functools.partial

    def partner_of(state, *levels):
        if levels[0] < narrow_bits:
            return swapped(state, "narrow", list(levels))
        return swapped(state, "wide", [level - narrow_bits for level in levels])

    def kernels_of(*pairs):
        shape = jax.ShapeDtypeStruct((len(pairs), 2, ROWS, SLOTS), f32)
        return call(bind(later_kernels, pairs), shape, ids, other_ids, weights, hi, lo)

    partner = partner_of(field, 0)
    ids_shape = jax.ShapeDtypeStruct((level_count, 2, 1, SLOTS), jnp.int32)
    weights = jnp.asarray(weight_tiles())
    hi, lo = call(
        table_kernel,
        (table_shape, table_shape),
        table,
        scratch=[
            pltpu.VMEM((2, RANK, RANK, RANK, 2, NTAB), f32),
            pltpu.VMEM((ROWS, NTAB), f32),
            pltpu.SemaphoreType.DMA((2 * RANK,)),
        ],
        space=HBM,
        limit=51 * MIB,
        moved=5 * MIB,
    )
    kern, acc, ids, other_ids = call(
        bind(first_kernel, other_flip),
        (kern_shape, state_shape, ids_shape, ids_shape),
        field,
        phase_ids,
        weights,
        hi,
        lo,
        scratch=[kern_scratch],
    )
    kerns = kernels_of((1, True), (2, True))
    state = call(join_first, tagged_shape, acc, kern, partner, ids)

    near, both, far = partner_of(state, 1), partner_of(state, 1, 2), partner_of(state, 2)
    mid_kerns = kernels_of((3, True), (4, True), (4, False))
    acc = call(bind(half_kernel, 1, 0, 0), state_shape, state, kerns)
    kern, other = call(
        bind(other_first, 1), (kern_shape, state_shape), far, weights, hi, lo, scratch=[kern_scratch]
    )
    other = call(bind(far_kernel, 1, (), 1), state_shape, other, kern, both, kerns, scratch=[state_scratch])
    state = call(
        bind(near_kernel, 1, 0, 1), state_shape, acc, other, kerns, kerns, near, scratch=[state_scratch]
    )

    partner = partner_of(state, 3)
    acc = call(bind(half_kernel, 1, 0, 0), state_shape, state, mid_kerns)
    state = call(bind(join_kernel, 1, 0), state_shape, acc, mid_kerns, partner)

    near, both, far = partner_of(state, 4), partner_of(state, 4, 5), partner_of(state, 5)
    kerns = kernels_of((5, True), (6, True))
    acc = call(bind(half_kernel, 0, 1, 0), state_shape, state, mid_kerns)
    other = call(bind(half_kernel, 0, 2, 0), state_shape, far, mid_kerns)
    other = call(bind(far_kernel, 0, (2, 1), 0), state_shape, other, mid_kerns, both, kerns, scratch=[state_scratch])
    state = call(
        bind(near_kernel, 0, 1, 0), state_shape, acc, other, mid_kerns, kerns, near, scratch=[state_scratch]
    )

    partner = partner_of(state, 6)
    acc = call(bind(half_kernel, 0, 1, 0), state_shape, state, kerns)
    return call(bind(join_kernel, 0, 1), jax.ShapeDtypeStruct(field.shape, f32), acc, kerns, partner)


def solution(mesh):
    in_specs = (P(None, None, None, ("wide", "narrow")), P(), P(None, None, "narrow", None))
    out_specs = P(None, None, None, ("wide", "narrow"))
    return jax.shard_map(
        per_device, mesh=mesh, in_specs=in_specs, out_specs=out_specs, check_vma=False
    )
```

```python
import functools

import jax
import jax.numpy as jnp
import numpy as np
from jax import lax
from jax.experimental import pallas as pl
from jax.experimental.pallas import tpu as pltpu
from jax.sharding import PartitionSpec as P

RANK = 5
POINTS = RANK * RANK
GATHERS = 4
SLOTS = 128
NTAB = 512
BLOCK = 64
ROWS = RANK * BLOCK

VMEM = pl.BlockSpec(memory_space=pltpu.VMEM)
HBM = pl.BlockSpec(memory_space=pltpu.HBM)
MIB = 1024 * 1024


def swapped(block, axis, bits):
    flip = sum(1 << bit for bit in bits)
    return lax.ppermute(block, axis, [(low, low ^ flip) for low in range(lax.axis_size(axis))])


def half_weights(order_count):
    cheb_nodes = 0.5 + 0.5 * np.cos(np.pi * (2 * np.arange(order_count) + 1) / (2 * order_count))
    result = np.zeros((2, order_count, order_count))
    for child_half in range(2):
        points = (cheb_nodes + child_half) / 2.0
        lagrange = np.ones((order_count, order_count))
        for column in range(order_count):
            for other_node in range(order_count):
                if other_node != column:
                    lagrange[:, column] *= (points - cheb_nodes[other_node]) / (
                        cheb_nodes[column] - cheb_nodes[other_node]
                    )
        result[child_half] = lagrange / np.sqrt(2.0 * np.mean(np.sum(lagrange * lagrange, axis=1)))
    return result


def weight_tiles():
    tiles = np.zeros((2, BLOCK, SLOTS), np.float32)
    tiles[:, : 2 * POINTS] = np.repeat(half_weights(RANK).reshape(2, POINTS, 1), 2, axis=1)
    return tiles


def point(parity, shared, moving):
    return moving * RANK + shared if parity == 0 else shared * RANK + moving


def level_bit(level):
    bits = lax.axis_size("narrow").bit_length() - 1
    if level < bits:
        return lax.axis_index("narrow") // 2**level % 2
    return lax.axis_index("wide") // 2 ** (level - bits) % 2


def turned(tile):
    return jnp.concatenate([-tile[GATHERS:], tile[:GATHERS]], axis=0)


def apply_side(parity, kern, source, start, finish):
    for shared in range(RANK):
        tiles = [source(point(parity, shared, v)) for v in range(RANK)]
        turns = [turned(t) for t in tiles]
        for u in range(RANK):
            total = start(point(parity, shared, u))
            for v in range(RANK):
                row = shared * BLOCK + 2 * (u * RANK + v)
                real = kern(row)
                imag = kern(row + 1)
                term = real * tiles[v] + imag * turns[v]
                total = term if total is None else total + term
            finish(point(parity, shared, u), total)


def gathered(first, second, bit, weights_ref, hi, lo):
    own = jnp.where(bit == 0, first, second)
    partner = jnp.where(bit == 0, second, first)
    entry = lax.broadcasted_iota(jnp.int32, (NTAB, SLOTS), 0)
    hot = jnp.concatenate(
        [jnp.where(entry == own, 1.0, 0.0), jnp.where(entry == partner, 1.0, 0.0)], axis=1
    ).astype(jnp.bfloat16)
    values = jnp.dot(hi, hot, preferred_element_type=jnp.float32) + jnp.dot(
        lo, hot, preferred_element_type=jnp.float32
    )
    weights = jnp.where(bit == 0, weights_ref[0], weights_ref[1])
    weights = jnp.concatenate([weights] * RANK, axis=0)
    return values[:, :SLOTS] * weights, values[:, SLOTS:] * weights


def kern_rows(ref, *lead):
    return lambda row: ref[lead + (pl.ds(row, 1), slice(None))]


def tiles_of(ref):
    if ref.shape[1] == POINTS:
        return lambda p: jnp.concatenate([ref[0, p], ref[1, p]], axis=0)
    return lambda p: ref[p]


def nothing(p):
    return None


def putter(ref):
    def put(p, tile):
        if ref.shape[1] == POINTS:
            ref[0, p] = tile[:GATHERS]
            ref[1, p] = tile[GATHERS:]
        else:
            ref[p] = tile

    return put


def table_kernel(table_hbm, hi_ref, lo_ref, table, flat, sems):
    copies = []
    for parity in range(2):
        for shared in range(RANK):
            if parity == 0:
                source = table_hbm.at[:, shared, :, shared]
            else:
                source = table_hbm.at[shared, :, shared, :]
            copies.append(pltpu.make_async_copy(source, table.at[parity, shared], sems.at[len(copies)]))
            copies[-1].start()
    for parity in range(2):
        for shared in range(RANK):
            tail = shared * BLOCK + 2 * POINTS
            flat[pl.ds(tail, BLOCK - 2 * POINTS)] = jnp.zeros((BLOCK - 2 * POINTS, NTAB), jnp.float32)
            copies[parity * RANK + shared].wait()
            for u in range(RANK):
                for v in range(RANK):
                    flat[pl.ds(shared * BLOCK + 2 * (u * RANK + v), 2)] = table[parity, shared, u, v]
        whole = flat[...]
        hi = whole.astype(jnp.bfloat16)
        hi_ref[parity] = hi
        lo_ref[parity] = (whole - hi.astype(jnp.float32)).astype(jnp.bfloat16)


def first_kernel(
    other_flip, field_ref, all_ids_ref, weights_ref, hi_ref, lo_ref, kern_ref, acc_ref, ids_ref, other_ref, own
):
    wide_index = lax.axis_index("wide")
    for device, ref in ((wide_index, ids_ref), (wide_index ^ other_flip, other_ref)):
        ref[...] = all_ids_ref[:, :, :, pl.ds(pl.multiple_of(device * SLOTS, SLOTS), SLOTS)]
    own[...], kern_ref[...] = gathered(
        ids_ref[0, 0], ids_ref[0, 1], level_bit(0), weights_ref, hi_ref[0], lo_ref[0]
    )
    apply_side(0, kern_rows(own), tiles_of(field_ref), nothing, putter(acc_ref))


def later_kernels(pairs, ids_ref, other_ref, weights_ref, hi_ref, lo_ref, kern_ref):
    for at, (level, mine) in enumerate(pairs):
        ids = ids_ref if mine else other_ref
        parity = level % 2
        kern_ref[at, 0], kern_ref[at, 1] = gathered(
            ids[level, 0], ids[level, 1], level_bit(level), weights_ref, hi_ref[parity], lo_ref[parity]
        )


def join_first(acc_ref, kern_ref, field_ref, ids_ref, out_ref):
    apply_side(0, kern_rows(kern_ref), tiles_of(field_ref), tiles_of(acc_ref), putter(out_ref))
    out_ref[POINTS] = jnp.concatenate(
        [ids_ref[1, s].astype(jnp.float32) for s in range(2)] + [jnp.zeros((6, SLOTS), jnp.float32)], axis=0
    )


def half_kernel(parity, at, side, state_ref, kern_ref, acc_ref):
    apply_side(parity, kern_rows(kern_ref, at, side), tiles_of(state_ref), nothing, putter(acc_ref))


def join_kernel(parity, at, acc_ref, kern_ref, state_ref, out_ref):
    apply_side(parity, kern_rows(kern_ref, at, 1), tiles_of(state_ref), tiles_of(acc_ref), putter(out_ref))


def last_kernel(parity, at, acc_ref, kern_ref, state_ref, out_hbm, out, sems):
    copies = []

    def put(p, tile):
        i, j = divmod(p, RANK)
        out[0, i, j] = tile[:GATHERS]
        out[1, i, j] = tile[GATHERS:]
        if i == RANK - 1:
            copies.append(pltpu.make_async_copy(out.at[:, :, j], out_hbm.at[:, :, j], sems.at[j]))
            copies[-1].start()

    apply_side(parity, kern_rows(kern_ref, at, 1), tiles_of(state_ref), tiles_of(acc_ref), put)
    for copy in copies:
        copy.wait()


def other_first(level, state_ref, weights_ref, hi_ref, lo_ref, kern_ref, acc_ref, own):
    parity = level % 2
    ids = state_ref[POINTS].astype(jnp.int32)
    own[...], kern_ref[...] = gathered(
        ids[0:1], ids[1:2], level_bit(level), weights_ref, hi_ref[parity], lo_ref[parity]
    )
    apply_side(parity, kern_rows(own), tiles_of(state_ref), nothing, putter(acc_ref))


def far_kernel(parity, kern_at, at, acc_ref, kern_ref, state_ref, kerns_ref, out_ref, mid):
    apply_side(parity, kern_rows(kern_ref, *kern_at), tiles_of(state_ref), tiles_of(acc_ref), putter(mid))
    apply_side(1 - parity, kern_rows(kerns_ref, at, 1), tiles_of(mid), nothing, putter(out_ref))


def near_kernel(parity, at, later, acc_ref, far_ref, kerns_ref, later_ref, state_ref, out_ref, mid):
    apply_side(parity, kern_rows(kerns_ref, at, 1), tiles_of(state_ref), tiles_of(acc_ref), putter(mid))
    apply_side(1 - parity, kern_rows(later_ref, later, 0), tiles_of(mid), tiles_of(far_ref), putter(out_ref))


def call(kernel, outs, *args, scratch=(), space=VMEM, out_space=VMEM, limit=40 * MIB, moved=MIB):
    return pl.pallas_call(
        kernel,
        out_shape=outs,
        in_specs=[space] * len(args),
        out_specs=jax.tree.map(lambda _: out_space, outs),
        scratch_shapes=scratch,
        compiler_params=pltpu.CompilerParams(vmem_limit_bytes=limit),
        cost_estimate=pl.CostEstimate(flops=2_000_000, bytes_accessed=moved, transcendentals=0),
    )(*args)


def per_device(field, phase_table, phase_ids):
    narrow_bits = lax.axis_size("narrow").bit_length() - 1
    level_count = phase_ids.shape[0]
    other_flip = 1 << 5 - narrow_bits
    table = phase_table.transpose(1, 2, 0, 3).reshape(RANK, RANK, RANK, RANK, 2, NTAB)
    f32 = jnp.float32
    state_shape = jax.ShapeDtypeStruct((POINTS, 2 * GATHERS, SLOTS), f32)
    tagged_shape = jax.ShapeDtypeStruct((POINTS + 1, 2 * GATHERS, SLOTS), f32)
    table_shape = jax.ShapeDtypeStruct((2, ROWS, NTAB), jnp.bfloat16)
    kern_shape = jax.ShapeDtypeStruct((ROWS, SLOTS), f32)
    state_scratch = pltpu.VMEM(state_shape.shape, f32)
    kern_scratch = pltpu.VMEM(kern_shape.shape, f32)
    bind = functools.partial

    def partner_of(state, *levels):
        if levels[0] < narrow_bits:
            return swapped(state, "narrow", list(levels))
        return swapped(state, "wide", [level - narrow_bits for level in levels])

    def kernels_of(*pairs):
        shape = jax.ShapeDtypeStruct((len(pairs), 2, ROWS, SLOTS), f32)
        return call(bind(later_kernels, pairs), shape, ids, other_ids, weights, hi, lo)

    partner = partner_of(field, 0)
    ids_shape = jax.ShapeDtypeStruct((level_count, 2, 1, SLOTS), jnp.int32)
    weights = jnp.asarray(weight_tiles())
    hi, lo = call(
        table_kernel,
        (table_shape, table_shape),
        table,
        scratch=[
            pltpu.VMEM((2, RANK, RANK, RANK, 2, NTAB), f32),
            pltpu.VMEM((ROWS, NTAB), f32),
            pltpu.SemaphoreType.DMA((2 * RANK,)),
        ],
        space=HBM,
        limit=51 * MIB,
        moved=5 * MIB,
    )
    kern, acc, ids, other_ids = call(
        bind(first_kernel, other_flip),
        (kern_shape, state_shape, ids_shape, ids_shape),
        field,
        phase_ids,
        weights,
        hi,
        lo,
        scratch=[kern_scratch],
    )
    kerns = kernels_of((1, True), (2, True))
    state = call(join_first, tagged_shape, acc, kern, partner, ids)

    near, both, far = partner_of(state, 1), partner_of(state, 1, 2), partner_of(state, 2)
    mid_kerns = kernels_of((3, True), (4, True), (4, False))
    acc = call(bind(half_kernel, 1, 0, 0), state_shape, state, kerns)
    kern, other = call(
        bind(other_first, 1), (kern_shape, state_shape), far, weights, hi, lo, scratch=[kern_scratch]
    )
    other = call(bind(far_kernel, 1, (), 1), state_shape, other, kern, both, kerns, scratch=[state_scratch])
    state = call(
        bind(near_kernel, 1, 0, 1), state_shape, acc, other, kerns, kerns, near, scratch=[state_scratch]
    )

    partner = partner_of(state, 3)
    acc = call(bind(half_kernel, 1, 0, 0), state_shape, state, mid_kerns)
    state = call(bind(join_kernel, 1, 0), state_shape, acc, mid_kerns, partner)

    near, both, far = partner_of(state, 4), partner_of(state, 4, 5), partner_of(state, 5)
    kerns = kernels_of((5, True), (6, True))
    acc = call(bind(half_kernel, 0, 1, 0), state_shape, state, mid_kerns)
    other = call(bind(half_kernel, 0, 2, 0), state_shape, far, mid_kerns)
    other = call(bind(far_kernel, 0, (2, 1), 0), state_shape, other, mid_kerns, both, kerns, scratch=[state_scratch])
    state = call(
        bind(near_kernel, 0, 1, 0), state_shape, acc, other, mid_kerns, kerns, near, scratch=[state_scratch]
    )

    partner = partner_of(state, 6)
    acc = call(bind(half_kernel, 0, 1, 0), state_shape, state, kerns)
    split_shape = (2, RANK, RANK, GATHERS, SLOTS)
    out = call(
        bind(last_kernel, 0, 1),
        jax.ShapeDtypeStruct(split_shape, f32),
        acc,
        kerns,
        partner,
        scratch=[pltpu.VMEM(split_shape, f32), pltpu.SemaphoreType.DMA((RANK,))],
        out_space=HBM,
    )
    return out.reshape(field.shape)


def solution(mesh):
    in_specs = (P(None, None, None, ("wide", "narrow")), P(), P(None, None, "narrow", None))
    out_specs = P(None, None, None, ("wide", "narrow"))
    return jax.shard_map(
        per_device, mesh=mesh, in_specs=in_specs, out_specs=out_specs, check_vma=False
    )
```

```python
import functools

import jax
import jax.numpy as jnp
import numpy as np
from jax import lax
from jax.experimental import pallas as pl
from jax.experimental.pallas import tpu as pltpu
from jax.sharding import PartitionSpec as P

RANK = 5
POINTS = RANK * RANK
GATHERS = 4
SLOTS = 128
NTAB = 512
BLOCK = 64
ROWS = RANK * BLOCK

VMEM = pl.BlockSpec(memory_space=pltpu.VMEM)
HBM = pl.BlockSpec(memory_space=pltpu.HBM)
MIB = 1024 * 1024
MOVED = 6 * MIB


def swapped(block, axis, bits):
    flip = sum(1 << bit for bit in bits)
    return lax.ppermute(block, axis, [(low, low ^ flip) for low in range(lax.axis_size(axis))])


def half_weights(order_count):
    cheb_nodes = 0.5 + 0.5 * np.cos(np.pi * (2 * np.arange(order_count) + 1) / (2 * order_count))
    result = np.zeros((2, order_count, order_count))
    for child_half in range(2):
        points = (cheb_nodes + child_half) / 2.0
        lagrange = np.ones((order_count, order_count))
        for column in range(order_count):
            for other_node in range(order_count):
                if other_node != column:
                    lagrange[:, column] *= (points - cheb_nodes[other_node]) / (
                        cheb_nodes[column] - cheb_nodes[other_node]
                    )
        result[child_half] = lagrange / np.sqrt(2.0 * np.mean(np.sum(lagrange * lagrange, axis=1)))
    return result


def weight_tiles():
    tiles = np.zeros((2, BLOCK, SLOTS), np.float32)
    tiles[:, : 2 * POINTS] = np.repeat(half_weights(RANK).reshape(2, POINTS, 1), 2, axis=1)
    return tiles


def point(parity, shared, moving):
    return moving * RANK + shared if parity == 0 else shared * RANK + moving


def level_bit(level):
    bits = lax.axis_size("narrow").bit_length() - 1
    if level < bits:
        return lax.axis_index("narrow") // 2**level % 2
    return lax.axis_index("wide") // 2 ** (level - bits) % 2


def turned(tile):
    return jnp.concatenate([-tile[GATHERS:], tile[:GATHERS]], axis=0)


def apply_side(parity, kern, source, start, finish):
    for shared in range(RANK):
        tiles = [source(point(parity, shared, v)) for v in range(RANK)]
        turns = [turned(t) for t in tiles]
        for u in range(RANK):
            total = start(point(parity, shared, u))
            for v in range(RANK):
                row = shared * BLOCK + 2 * (u * RANK + v)
                real = kern(row)
                imag = kern(row + 1)
                term = real * tiles[v] + imag * turns[v]
                total = term if total is None else total + term
            finish(point(parity, shared, u), total)


def gathered(first, second, bit, weights_ref, hi, lo):
    own = jnp.where(bit == 0, first, second)
    partner = jnp.where(bit == 0, second, first)
    entry = lax.broadcasted_iota(jnp.int32, (NTAB, SLOTS), 0)
    hot = jnp.concatenate(
        [jnp.where(entry == own, 1.0, 0.0), jnp.where(entry == partner, 1.0, 0.0)], axis=1
    ).astype(jnp.bfloat16)
    values = jnp.dot(hi, hot, preferred_element_type=jnp.float32) + jnp.dot(
        lo, hot, preferred_element_type=jnp.float32
    )
    weights = jnp.where(bit == 0, weights_ref[0], weights_ref[1])
    weights = jnp.concatenate([weights] * RANK, axis=0)
    return values[:, :SLOTS] * weights, values[:, SLOTS:] * weights


def kern_rows(ref, *lead):
    return lambda row: ref[lead + (pl.ds(row, 1), slice(None))]


def tiles_of(ref):
    if ref.shape[1] == POINTS:
        return lambda p: jnp.concatenate([ref[0, p], ref[1, p]], axis=0)
    return lambda p: ref[p]


def nothing(p):
    return None


def putter(ref):
    def put(p, tile):
        if ref.shape[1] == POINTS:
            ref[0, p] = tile[:GATHERS]
            ref[1, p] = tile[GATHERS:]
        else:
            ref[p] = tile

    return put


def table_kernel(table_hbm, hi_ref, lo_ref, table, flat, sems):
    copies = []
    for parity in range(2):
        for shared in range(RANK):
            if parity == 0:
                source = table_hbm.at[:, shared, :, shared]
            else:
                source = table_hbm.at[shared, :, shared, :]
            copies.append(pltpu.make_async_copy(source, table.at[parity, shared], sems.at[len(copies)]))
            copies[-1].start()
    for parity in range(2):
        for shared in range(RANK):
            tail = shared * BLOCK + 2 * POINTS
            flat[pl.ds(tail, BLOCK - 2 * POINTS)] = jnp.zeros((BLOCK - 2 * POINTS, NTAB), jnp.float32)
            copies[parity * RANK + shared].wait()
            for u in range(RANK):
                for v in range(RANK):
                    flat[pl.ds(shared * BLOCK + 2 * (u * RANK + v), 2)] = table[parity, shared, u, v]
        whole = flat[...]
        hi = whole.astype(jnp.bfloat16)
        hi_ref[parity] = hi
        lo_ref[parity] = (whole - hi.astype(jnp.float32)).astype(jnp.bfloat16)


def first_kernel(
    other_flip, field_ref, all_ids_ref, weights_ref, hi_ref, lo_ref,
    kern_ref, acc_ref, ids_ref, other_ref, next_ref, own,
):
    wide_index = lax.axis_index("wide")
    for device, ref in ((wide_index, ids_ref), (wide_index ^ other_flip, other_ref)):
        ref[...] = all_ids_ref[:, :, :, pl.ds(pl.multiple_of(device * SLOTS, SLOTS), SLOTS)]
    own[...], kern_ref[...] = gathered(
        ids_ref[0, 0], ids_ref[0, 1], level_bit(0), weights_ref, hi_ref[0], lo_ref[0]
    )
    apply_side(0, kern_rows(own), tiles_of(field_ref), nothing, putter(acc_ref))
    later_kernels(((1, True), (2, True)), ids_ref, other_ref, weights_ref, hi_ref, lo_ref, next_ref)


def later_kernels(pairs, ids_ref, other_ref, weights_ref, hi_ref, lo_ref, kern_ref):
    for at, (level, mine) in enumerate(pairs):
        ids = ids_ref if mine else other_ref
        parity = level % 2
        kern_ref[at, 0], kern_ref[at, 1] = gathered(
            ids[level, 0], ids[level, 1], level_bit(level), weights_ref, hi_ref[parity], lo_ref[parity]
        )


def join_first(acc_ref, kern_ref, field_ref, ids_ref, out_ref):
    apply_side(0, kern_rows(kern_ref), tiles_of(field_ref), tiles_of(acc_ref), putter(out_ref))
    out_ref[POINTS] = jnp.concatenate(
        [ids_ref[1, s].astype(jnp.float32) for s in range(2)] + [jnp.zeros((6, SLOTS), jnp.float32)], axis=0
    )


def half_kernel(parity, at, side, state_ref, kern_ref, acc_ref):
    apply_side(parity, kern_rows(kern_ref, at, side), tiles_of(state_ref), nothing, putter(acc_ref))


def half_and_copy(parity, at, state_ref, kern_ref, acc_ref, copy_ref):
    copy_ref[...] = state_ref[:POINTS]
    apply_side(parity, kern_rows(kern_ref, at, 0), tiles_of(state_ref), nothing, putter(acc_ref))


def near_early(parity, at, later, acc_ref, kerns_ref, state_ref, other_ref, out_ref, same_ref, mid):
    apply_side(parity, kern_rows(kerns_ref, at, 1), tiles_of(state_ref), tiles_of(acc_ref), putter(mid))
    apply_side(1 - parity, kern_rows(kerns_ref, later, 0), tiles_of(mid), nothing, putter(out_ref))
    same_ref[...] = other_ref[...]


def far_late(parity, kern_at, at, acc_ref, kern_ref, state_ref, kerns_ref, near_ref, out_ref, mid):
    apply_side(parity, kern_rows(kern_ref, *kern_at), tiles_of(state_ref), tiles_of(acc_ref), putter(mid))
    apply_side(1 - parity, kern_rows(kerns_ref, at, 1), tiles_of(mid), tiles_of(near_ref), putter(out_ref))


def join_kernel(parity, at, acc_ref, kern_ref, state_ref, out_ref):
    apply_side(parity, kern_rows(kern_ref, at, 1), tiles_of(state_ref), tiles_of(acc_ref), putter(out_ref))


def other_first(level, state_ref, weights_ref, hi_ref, lo_ref, kern_ref, acc_ref, own):
    parity = level % 2
    ids = state_ref[POINTS].astype(jnp.int32)
    own[...], kern_ref[...] = gathered(
        ids[0:1], ids[1:2], level_bit(level), weights_ref, hi_ref[parity], lo_ref[parity]
    )
    apply_side(parity, kern_rows(own), tiles_of(state_ref), nothing, putter(acc_ref))


def far_kernel(parity, kern_at, at, acc_ref, kern_ref, state_ref, kerns_ref, out_ref, mid):
    apply_side(parity, kern_rows(kern_ref, *kern_at), tiles_of(state_ref), tiles_of(acc_ref), putter(mid))
    apply_side(1 - parity, kern_rows(kerns_ref, at, 1), tiles_of(mid), nothing, putter(out_ref))


def near_kernel(parity, at, later, acc_ref, far_ref, kerns_ref, later_ref, state_ref, out_ref, mid):
    apply_side(parity, kern_rows(kerns_ref, at, 1), tiles_of(state_ref), tiles_of(acc_ref), putter(mid))
    apply_side(1 - parity, kern_rows(later_ref, later, 0), tiles_of(mid), tiles_of(far_ref), putter(out_ref))


def call(kernel, outs, *args, scratch=(), space=VMEM, limit=40 * MIB, moved=MIB):
    return pl.pallas_call(
        kernel,
        out_shape=outs,
        in_specs=[space] * len(args),
        out_specs=jax.tree.map(lambda _: VMEM, outs),
        scratch_shapes=scratch,
        compiler_params=pltpu.CompilerParams(vmem_limit_bytes=limit),
        cost_estimate=pl.CostEstimate(flops=2_000_000, bytes_accessed=moved, transcendentals=0),
    )(*args)


def per_device(field, phase_table, phase_ids):
    narrow_bits = lax.axis_size("narrow").bit_length() - 1
    level_count = phase_ids.shape[0]
    other_flip = 1 << 5 - narrow_bits
    table = phase_table.transpose(1, 2, 0, 3).reshape(RANK, RANK, RANK, RANK, 2, NTAB)
    f32 = jnp.float32
    state_shape = jax.ShapeDtypeStruct((POINTS, 2 * GATHERS, SLOTS), f32)
    tagged_shape = jax.ShapeDtypeStruct((POINTS + 1, 2 * GATHERS, SLOTS), f32)
    table_shape = jax.ShapeDtypeStruct((2, ROWS, NTAB), jnp.bfloat16)
    kern_shape = jax.ShapeDtypeStruct((ROWS, SLOTS), f32)
    state_scratch = pltpu.VMEM(state_shape.shape, f32)
    kern_scratch = pltpu.VMEM(kern_shape.shape, f32)
    bind = functools.partial

    def partner_of(state, *levels):
        if levels[0] < narrow_bits:
            return swapped(state, "narrow", list(levels))
        return swapped(state, "wide", [level - narrow_bits for level in levels])

    def kernels_of(*pairs):
        shape = jax.ShapeDtypeStruct((len(pairs), 2, ROWS, SLOTS), f32)
        return call(bind(later_kernels, pairs), shape, ids, other_ids, weights, hi, lo)

    partner = partner_of(field, 0)
    ids_shape = jax.ShapeDtypeStruct((level_count, 2, 1, SLOTS), jnp.int32)
    weights = jnp.asarray(weight_tiles())
    hi, lo = call(
        table_kernel,
        (table_shape, table_shape),
        table,
        scratch=[
            pltpu.VMEM((2, RANK, RANK, RANK, 2, NTAB), f32),
            pltpu.VMEM((ROWS, NTAB), f32),
            pltpu.SemaphoreType.DMA((2 * RANK,)),
        ],
        space=HBM,
        limit=51 * MIB,
        moved=5 * MIB,
    )
    kern, acc, ids, other_ids, kerns = call(
        bind(first_kernel, other_flip),
        (kern_shape, state_shape, ids_shape, ids_shape, jax.ShapeDtypeStruct((2, 2, ROWS, SLOTS), f32)),
        field,
        phase_ids,
        weights,
        hi,
        lo,
        scratch=[kern_scratch],
    )
    state = call(join_first, tagged_shape, acc, kern, partner, ids)

    both, far = partner_of(state, 1, 2), partner_of(state, 2)
    acc, again = call(bind(half_and_copy, 1, 0), (state_shape, state_shape), state, kerns, moved=MOVED)
    near = partner_of(again, 1)
    mid_kerns = kernels_of((3, True), (4, True), (4, False))
    kern, other = call(
        bind(other_first, 1), (kern_shape, state_shape), far, weights, hi, lo, scratch=[kern_scratch]
    )
    acc, other = call(
        bind(near_early, 1, 0, 1), (state_shape, state_shape), acc, kerns, near, other, scratch=[state_scratch]
    )
    state = call(bind(far_late, 1, (), 1), state_shape, other, kern, both, kerns, acc, scratch=[state_scratch])

    partner = partner_of(state, 3)
    acc = call(bind(half_kernel, 1, 0, 0), state_shape, state, mid_kerns)
    state = call(bind(join_kernel, 1, 0), state_shape, acc, mid_kerns, partner)

    near, both, far = partner_of(state, 4), partner_of(state, 4, 5), partner_of(state, 5)
    kerns = kernels_of((5, True), (6, True))
    acc = call(bind(half_kernel, 0, 1, 0), state_shape, state, mid_kerns)
    other = call(bind(half_kernel, 0, 2, 0), state_shape, far, mid_kerns)
    other = call(bind(far_kernel, 0, (2, 1), 0), state_shape, other, mid_kerns, both, kerns, scratch=[state_scratch])
    state = call(
        bind(near_kernel, 0, 1, 0), state_shape, acc, other, mid_kerns, kerns, near, scratch=[state_scratch]
    )

    partner = partner_of(state, 6)
    acc = call(bind(half_kernel, 0, 1, 0), state_shape, state, kerns)
    return call(bind(join_kernel, 0, 1), jax.ShapeDtypeStruct(field.shape, f32), acc, kerns, partner)


def solution(mesh):
    in_specs = (P(None, None, None, ("wide", "narrow")), P(), P(None, None, "narrow", None))
    out_specs = P(None, None, None, ("wide", "narrow"))
    return jax.shard_map(
        per_device, mesh=mesh, in_specs=in_specs, out_specs=out_specs, check_vma=False
    )
```

```python
import functools

import jax
import jax.numpy as jnp
import numpy as np
from jax import lax
from jax.experimental import pallas as pl
from jax.experimental.pallas import tpu as pltpu
from jax.sharding import PartitionSpec as P

RANK = 5
POINTS = RANK * RANK
GATHERS = 4
SLOTS = 128
NTAB = 512
BLOCK = 64
ROWS = RANK * BLOCK

VMEM = pl.BlockSpec(memory_space=pltpu.VMEM)
HBM = pl.BlockSpec(memory_space=pltpu.HBM)
MIB = 1024 * 1024


def swapped(block, axis, bits):
    flip = sum(1 << bit for bit in bits)
    return lax.ppermute(block, axis, [(low, low ^ flip) for low in range(lax.axis_size(axis))])


def half_weights(order_count):
    cheb_nodes = 0.5 + 0.5 * np.cos(np.pi * (2 * np.arange(order_count) + 1) / (2 * order_count))
    result = np.zeros((2, order_count, order_count))
    for child_half in range(2):
        points = (cheb_nodes + child_half) / 2.0
        lagrange = np.ones((order_count, order_count))
        for column in range(order_count):
            for other_node in range(order_count):
                if other_node != column:
                    lagrange[:, column] *= (points - cheb_nodes[other_node]) / (
                        cheb_nodes[column] - cheb_nodes[other_node]
                    )
        result[child_half] = lagrange / np.sqrt(2.0 * np.mean(np.sum(lagrange * lagrange, axis=1)))
    return result


def weight_tiles():
    tiles = np.zeros((2, BLOCK, SLOTS), np.float32)
    tiles[:, : 2 * POINTS] = np.repeat(half_weights(RANK).reshape(2, POINTS, 1), 2, axis=1)
    return tiles


def point(parity, shared, moving):
    return moving * RANK + shared if parity == 0 else shared * RANK + moving


def level_bit(level):
    bits = lax.axis_size("narrow").bit_length() - 1
    if level < bits:
        return lax.axis_index("narrow") // 2**level % 2
    return lax.axis_index("wide") // 2 ** (level - bits) % 2


def turned(tile):
    return jnp.concatenate([-tile[GATHERS:], tile[:GATHERS]], axis=0)


def apply_side(parity, kern, source, start, finish):
    for shared in range(RANK):
        tiles = [source(point(parity, shared, v)) for v in range(RANK)]
        turns = [turned(t) for t in tiles]
        for u in range(RANK):
            total = start(point(parity, shared, u))
            for v in range(RANK):
                row = shared * BLOCK + 2 * (u * RANK + v)
                real = kern(row)
                imag = kern(row + 1)
                term = real * tiles[v] + imag * turns[v]
                total = term if total is None else total + term
            finish(point(parity, shared, u), total)


def gathered(first, second, bit, weights_ref, hi, lo):
    own = jnp.where(bit == 0, first, second)
    partner = jnp.where(bit == 0, second, first)
    entry = lax.broadcasted_iota(jnp.int32, (NTAB, SLOTS), 0)
    hot = jnp.concatenate(
        [jnp.where(entry == own, 1.0, 0.0), jnp.where(entry == partner, 1.0, 0.0)], axis=1
    ).astype(jnp.bfloat16)
    values = jnp.dot(hi, hot, preferred_element_type=jnp.float32) + jnp.dot(
        lo, hot, preferred_element_type=jnp.float32
    )
    weights = jnp.where(bit == 0, weights_ref[0], weights_ref[1])
    weights = jnp.concatenate([weights] * RANK, axis=0)
    return values[:, :SLOTS] * weights, values[:, SLOTS:] * weights


def kern_rows(ref, *lead):
    return lambda row: ref[lead + (pl.ds(row, 1), slice(None))]


def tiles_of(ref):
    if ref.shape[1] == POINTS:
        return lambda p: jnp.concatenate([ref[0, p], ref[1, p]], axis=0)
    return lambda p: ref[p]


def nothing(p):
    return None


def putter(ref):
    def put(p, tile):
        if ref.shape[1] == POINTS:
            ref[0, p] = tile[:GATHERS]
            ref[1, p] = tile[GATHERS:]
        else:
            ref[p] = tile

    return put


def table_kernel(table_hbm, hi_ref, lo_ref, table, flat, sems):
    copies = []
    for parity in range(2):
        for shared in range(RANK):
            if parity == 0:
                source = table_hbm.at[:, shared, :, shared]
            else:
                source = table_hbm.at[shared, :, shared, :]
            copies.append(pltpu.make_async_copy(source, table.at[parity, shared], sems.at[len(copies)]))
    for copy in copies[:RANK]:
        copy.start()
    for parity in range(2):
        for shared in range(RANK):
            tail = shared * BLOCK + 2 * POINTS
            flat[pl.ds(tail, BLOCK - 2 * POINTS)] = jnp.zeros((BLOCK - 2 * POINTS, NTAB), jnp.float32)
            copies[parity * RANK + shared].wait()
            for u in range(RANK):
                for v in range(RANK):
                    flat[pl.ds(shared * BLOCK + 2 * (u * RANK + v), 2)] = table[parity, shared, u, v]
        if parity == 0:
            for copy in copies[RANK:]:
                copy.start()
        whole = flat[...]
        hi = whole.astype(jnp.bfloat16)
        hi_ref[parity] = hi
        lo_ref[parity] = (whole - hi.astype(jnp.float32)).astype(jnp.bfloat16)


def first_kernel(
    other_flip, field_ref, all_ids_ref, weights_ref, hi_ref, lo_ref, kern_ref, acc_ref, ids_ref, other_ref, own
):
    wide_index = lax.axis_index("wide")
    for device, ref in ((wide_index, ids_ref), (wide_index ^ other_flip, other_ref)):
        ref[...] = all_ids_ref[:, :, :, pl.ds(pl.multiple_of(device * SLOTS, SLOTS), SLOTS)]
    own[...], kern_ref[...] = gathered(
        ids_ref[0, 0], ids_ref[0, 1], level_bit(0), weights_ref, hi_ref[0], lo_ref[0]
    )
    apply_side(0, kern_rows(own), tiles_of(field_ref), nothing, putter(acc_ref))


def later_kernels(pairs, ids_ref, other_ref, weights_ref, hi_ref, lo_ref, kern_ref):
    for at, (level, mine) in enumerate(pairs):
        ids = ids_ref if mine else other_ref
        parity = level % 2
        kern_ref[at, 0], kern_ref[at, 1] = gathered(
            ids[level, 0], ids[level, 1], level_bit(level), weights_ref, hi_ref[parity], lo_ref[parity]
        )


def join_first(acc_ref, kern_ref, field_ref, ids_ref, out_ref):
    apply_side(0, kern_rows(kern_ref), tiles_of(field_ref), tiles_of(acc_ref), putter(out_ref))
    out_ref[POINTS] = jnp.concatenate(
        [ids_ref[1, s].astype(jnp.float32) for s in range(2)] + [jnp.zeros((6, SLOTS), jnp.float32)], axis=0
    )


def half_kernel(parity, at, side, state_ref, kern_ref, acc_ref):
    apply_side(parity, kern_rows(kern_ref, at, side), tiles_of(state_ref), nothing, putter(acc_ref))


def join_kernel(parity, at, acc_ref, kern_ref, state_ref, out_ref):
    apply_side(parity, kern_rows(kern_ref, at, 1), tiles_of(state_ref), tiles_of(acc_ref), putter(out_ref))


def other_first(level, state_ref, weights_ref, hi_ref, lo_ref, kern_ref, acc_ref, own):
    parity = level % 2
    ids = state_ref[POINTS].astype(jnp.int32)
    own[...], kern_ref[...] = gathered(
        ids[0:1], ids[1:2], level_bit(level), weights_ref, hi_ref[parity], lo_ref[parity]
    )
    apply_side(parity, kern_rows(own), tiles_of(state_ref), nothing, putter(acc_ref))


def far_kernel(parity, kern_at, at, acc_ref, kern_ref, state_ref, kerns_ref, out_ref, mid):
    apply_side(parity, kern_rows(kern_ref, *kern_at), tiles_of(state_ref), tiles_of(acc_ref), putter(mid))
    apply_side(1 - parity, kern_rows(kerns_ref, at, 1), tiles_of(mid), nothing, putter(out_ref))


def near_kernel(parity, at, later, acc_ref, far_ref, kerns_ref, state_ref, out_ref, mid):
    apply_side(parity, kern_rows(kerns_ref, at, 1), tiles_of(state_ref), tiles_of(acc_ref), putter(mid))
    apply_side(1 - parity, kern_rows(kerns_ref, later, 0), tiles_of(mid), tiles_of(far_ref), putter(out_ref))


def call(kernel, outs, *args, scratch=(), space=VMEM, limit=40 * MIB, moved=MIB):
    return pl.pallas_call(
        kernel,
        out_shape=outs,
        in_specs=[space] * len(args),
        out_specs=jax.tree.map(lambda _: VMEM, outs),
        scratch_shapes=scratch,
        compiler_params=pltpu.CompilerParams(vmem_limit_bytes=limit),
        cost_estimate=pl.CostEstimate(flops=2_000_000, bytes_accessed=moved, transcendentals=0),
    )(*args)


def per_device(field, phase_table, phase_ids):
    narrow_bits = lax.axis_size("narrow").bit_length() - 1
    level_count = phase_ids.shape[0]
    other_flip = 1 << 5 - narrow_bits
    table = phase_table.transpose(1, 2, 0, 3).reshape(RANK, RANK, RANK, RANK, 2, NTAB)
    f32 = jnp.float32
    state_shape = jax.ShapeDtypeStruct((POINTS, 2 * GATHERS, SLOTS), f32)
    tagged_shape = jax.ShapeDtypeStruct((POINTS + 1, 2 * GATHERS, SLOTS), f32)
    table_shape = jax.ShapeDtypeStruct((2, ROWS, NTAB), jnp.bfloat16)
    kern_shape = jax.ShapeDtypeStruct((ROWS, SLOTS), f32)
    state_scratch = pltpu.VMEM(state_shape.shape, f32)
    kern_scratch = pltpu.VMEM(kern_shape.shape, f32)
    bind = functools.partial

    def partner_of(state, *levels):
        if levels[0] < narrow_bits:
            return swapped(state, "narrow", list(levels))
        return swapped(state, "wide", [level - narrow_bits for level in levels])

    partner = partner_of(field, 0)
    ids_shape = jax.ShapeDtypeStruct((level_count, 2, 1, SLOTS), jnp.int32)
    weights = jnp.asarray(weight_tiles())
    hi, lo = call(
        table_kernel,
        (table_shape, table_shape),
        table,
        scratch=[
            pltpu.VMEM((2, RANK, RANK, RANK, 2, NTAB), f32),
            pltpu.VMEM((ROWS, NTAB), f32),
            pltpu.SemaphoreType.DMA((2 * RANK,)),
        ],
        space=HBM,
        limit=51 * MIB,
        moved=5 * MIB,
    )
    kern, acc, ids, other_ids = call(
        bind(first_kernel, other_flip),
        (kern_shape, state_shape, ids_shape, ids_shape),
        field,
        phase_ids,
        weights,
        hi,
        lo,
        scratch=[kern_scratch],
    )
    state = call(join_first, tagged_shape, acc, kern, partner, ids)

    near, both, far = partner_of(state, 1), partner_of(state, 1, 2), partner_of(state, 2)
    pairs = ((1, True), (2, True), (3, True), (4, True), (4, False), (5, True), (6, True))
    kerns = call(
        bind(later_kernels, pairs),
        jax.ShapeDtypeStruct((len(pairs), 2, ROWS, SLOTS), f32),
        ids,
        other_ids,
        weights,
        hi,
        lo,
    )
    acc = call(bind(half_kernel, 1, 0, 0), state_shape, state, kerns)
    kern, other = call(
        bind(other_first, 1), (kern_shape, state_shape), far, weights, hi, lo, scratch=[kern_scratch]
    )
    other = call(bind(far_kernel, 1, (), 1), state_shape, other, kern, both, kerns, scratch=[state_scratch])
    state = call(bind(near_kernel, 1, 0, 1), state_shape, acc, other, kerns, near, scratch=[state_scratch])

    partner = partner_of(state, 3)
    acc = call(bind(half_kernel, 1, 2, 0), state_shape, state, kerns)
    state = call(bind(join_kernel, 1, 2), state_shape, acc, kerns, partner)

    near, both, far = partner_of(state, 4), partner_of(state, 4, 5), partner_of(state, 5)
    acc = call(bind(half_kernel, 0, 3, 0), state_shape, state, kerns)
    other = call(bind(half_kernel, 0, 4, 0), state_shape, far, kerns)
    other = call(bind(far_kernel, 0, (4, 1), 5), state_shape, other, kerns, both, kerns, scratch=[state_scratch])
    state = call(bind(near_kernel, 0, 3, 5), state_shape, acc, other, kerns, near, scratch=[state_scratch])

    partner = partner_of(state, 6)
    acc = call(bind(half_kernel, 0, 6, 0), state_shape, state, kerns)
    return call(bind(join_kernel, 0, 6), jax.ShapeDtypeStruct(field.shape, f32), acc, kerns, partner)


def solution(mesh):
    in_specs = (P(None, None, None, ("wide", "narrow")), P(), P(None, None, "narrow", None))
    out_specs = P(None, None, None, ("wide", "narrow"))
    return jax.shard_map(
        per_device, mesh=mesh, in_specs=in_specs, out_specs=out_specs, check_vma=False
    )
```

```python
import functools

import jax
import jax.numpy as jnp
import numpy as np
from jax import lax
from jax.experimental import pallas as pl
from jax.experimental.pallas import tpu as pltpu
from jax.sharding import PartitionSpec as P

RANK = 5
POINTS = RANK * RANK
GATHERS = 4
SLOTS = 128
NTAB = 512
BLOCK = 64
ROWS = RANK * BLOCK

VMEM = pl.BlockSpec(memory_space=pltpu.VMEM)
HBM = pl.BlockSpec(memory_space=pltpu.HBM)
MIB = 1024 * 1024


def swapped(block, axis, bits):
    flip = sum(1 << bit for bit in bits)
    return lax.ppermute(block, axis, [(low, low ^ flip) for low in range(lax.axis_size(axis))])


def half_weights(order_count):
    cheb_nodes = 0.5 + 0.5 * np.cos(np.pi * (2 * np.arange(order_count) + 1) / (2 * order_count))
    result = np.zeros((2, order_count, order_count))
    for child_half in range(2):
        points = (cheb_nodes + child_half) / 2.0
        lagrange = np.ones((order_count, order_count))
        for column in range(order_count):
            for other_node in range(order_count):
                if other_node != column:
                    lagrange[:, column] *= (points - cheb_nodes[other_node]) / (
                        cheb_nodes[column] - cheb_nodes[other_node]
                    )
        result[child_half] = lagrange / np.sqrt(2.0 * np.mean(np.sum(lagrange * lagrange, axis=1)))
    return result


def weight_tiles():
    tiles = np.zeros((2, BLOCK, SLOTS), np.float32)
    tiles[:, : 2 * POINTS] = np.repeat(half_weights(RANK).reshape(2, POINTS, 1), 2, axis=1)
    return tiles


def point(parity, shared, moving):
    return moving * RANK + shared if parity == 0 else shared * RANK + moving


def level_bit(level):
    bits = lax.axis_size("narrow").bit_length() - 1
    if level < bits:
        return lax.axis_index("narrow") // 2**level % 2
    return lax.axis_index("wide") // 2 ** (level - bits) % 2


def turned(tile):
    return jnp.concatenate([-tile[GATHERS:], tile[:GATHERS]], axis=0)


def apply_side(parity, kern, source, start, finish):
    for shared in range(RANK):
        tiles = [source(point(parity, shared, v)) for v in range(RANK)]
        turns = [turned(t) for t in tiles]
        for u in range(RANK):
            total = start(point(parity, shared, u))
            for v in range(RANK):
                row = shared * BLOCK + 2 * (u * RANK + v)
                real = kern(row)
                imag = kern(row + 1)
                term = real * tiles[v] + imag * turns[v]
                total = term if total is None else total + term
            finish(point(parity, shared, u), total)


def gathered(first, second, bit, weights_ref, hi, lo):
    own = jnp.where(bit == 0, first, second)
    partner = jnp.where(bit == 0, second, first)
    entry = lax.broadcasted_iota(jnp.int32, (NTAB, SLOTS), 0)
    hot = jnp.concatenate(
        [jnp.where(entry == own, 1.0, 0.0), jnp.where(entry == partner, 1.0, 0.0)], axis=1
    ).astype(jnp.bfloat16)
    values = jnp.dot(hi, hot, preferred_element_type=jnp.float32) + jnp.dot(
        lo, hot, preferred_element_type=jnp.float32
    )
    weights = jnp.where(bit == 0, weights_ref[0], weights_ref[1])
    weights = jnp.concatenate([weights] * RANK, axis=0)
    return values[:, :SLOTS] * weights, values[:, SLOTS:] * weights


def kern_rows(ref, *lead):
    return lambda row: ref[lead + (pl.ds(row, 1), slice(None))]


def tiles_of(ref):
    if ref.shape[1] == POINTS:
        return lambda p: jnp.concatenate([ref[0, p], ref[1, p]], axis=0)
    return lambda p: ref[p]


def nothing(p):
    return None


def putter(ref):
    def put(p, tile):
        if ref.shape[1] == POINTS:
            ref[0, p] = tile[:GATHERS]
            ref[1, p] = tile[GATHERS:]
        else:
            ref[p] = tile

    return put


def table_kernel(table_hbm, hi_ref, lo_ref, table, flat, sems):
    copies = []
    for parity in range(2):
        for shared in range(RANK):
            if parity == 0:
                source = table_hbm.at[:, shared, :, shared]
            else:
                source = table_hbm.at[shared, :, shared, :]
            copies.append(pltpu.make_async_copy(source, table.at[parity, shared], sems.at[len(copies)]))
            copies[-1].start()
    for parity in range(2):
        for shared in range(RANK):
            tail = shared * BLOCK + 2 * POINTS
            flat[pl.ds(tail, BLOCK - 2 * POINTS)] = jnp.zeros((BLOCK - 2 * POINTS, NTAB), jnp.float32)
            copies[parity * RANK + shared].wait()
            for u in range(RANK):
                for v in range(RANK):
                    flat[pl.ds(shared * BLOCK + 2 * (u * RANK + v), 2)] = table[parity, shared, u, v]
        whole = flat[...]
        hi = whole.astype(jnp.bfloat16)
        hi_ref[parity] = hi
        lo_ref[parity] = (whole - hi.astype(jnp.float32)).astype(jnp.bfloat16)


def first_kernel(
    other_flip, field_ref, all_ids_ref, weights_ref, hi_ref, lo_ref, kern_ref, acc_ref, ids_ref, other_ref, own
):
    wide_index = lax.axis_index("wide")
    for device, ref in ((wide_index, ids_ref), (wide_index ^ other_flip, other_ref)):
        ref[...] = all_ids_ref[:, :, :, pl.ds(pl.multiple_of(device * SLOTS, SLOTS), SLOTS)]
    own[...], kern_ref[...] = gathered(
        ids_ref[0, 0], ids_ref[0, 1], level_bit(0), weights_ref, hi_ref[0], lo_ref[0]
    )
    apply_side(0, kern_rows(own), tiles_of(field_ref), nothing, putter(acc_ref))


def later_kernels(pairs, ids_ref, other_ref, weights_ref, hi_ref, lo_ref, kern_ref):
    for at, (level, mine) in enumerate(pairs):
        ids = ids_ref if mine else other_ref
        parity = level % 2
        kern_ref[at, 0], kern_ref[at, 1] = gathered(
            ids[level, 0], ids[level, 1], level_bit(level), weights_ref, hi_ref[parity], lo_ref[parity]
        )


def join_first(acc_ref, kern_ref, field_ref, ids_ref, out_ref, tagged_ref):
    def put(p, tile):
        out_ref[p] = tile
        tagged_ref[p] = tile

    apply_side(0, kern_rows(kern_ref), tiles_of(field_ref), tiles_of(acc_ref), put)
    tagged_ref[POINTS] = jnp.concatenate(
        [ids_ref[1, s].astype(jnp.float32) for s in range(2)] + [jnp.zeros((6, SLOTS), jnp.float32)], axis=0
    )


def half_kernel(parity, at, side, state_ref, kern_ref, acc_ref):
    apply_side(parity, kern_rows(kern_ref, at, side), tiles_of(state_ref), nothing, putter(acc_ref))


def join_kernel(parity, at, acc_ref, kern_ref, state_ref, out_ref):
    apply_side(parity, kern_rows(kern_ref, at, 1), tiles_of(state_ref), tiles_of(acc_ref), putter(out_ref))


def other_first(level, state_ref, weights_ref, hi_ref, lo_ref, kern_ref, acc_ref, own):
    parity = level % 2
    ids = state_ref[POINTS].astype(jnp.int32)
    own[...], kern_ref[...] = gathered(
        ids[0:1], ids[1:2], level_bit(level), weights_ref, hi_ref[parity], lo_ref[parity]
    )
    apply_side(parity, kern_rows(own), tiles_of(state_ref), nothing, putter(acc_ref))


def far_kernel(parity, kern_at, at, acc_ref, kern_ref, state_ref, kerns_ref, out_ref, mid):
    apply_side(parity, kern_rows(kern_ref, *kern_at), tiles_of(state_ref), tiles_of(acc_ref), putter(mid))
    apply_side(1 - parity, kern_rows(kerns_ref, at, 1), tiles_of(mid), nothing, putter(out_ref))


def near_kernel(parity, at, later, acc_ref, far_ref, kerns_ref, state_ref, out_ref, mid):
    apply_side(parity, kern_rows(kerns_ref, at, 1), tiles_of(state_ref), tiles_of(acc_ref), putter(mid))
    apply_side(1 - parity, kern_rows(kerns_ref, later, 0), tiles_of(mid), tiles_of(far_ref), putter(out_ref))


def call(kernel, outs, *args, scratch=(), space=VMEM, limit=40 * MIB, moved=MIB):
    return pl.pallas_call(
        kernel,
        out_shape=outs,
        in_specs=[space] * len(args),
        out_specs=jax.tree.map(lambda _: VMEM, outs),
        scratch_shapes=scratch,
        compiler_params=pltpu.CompilerParams(vmem_limit_bytes=limit),
        cost_estimate=pl.CostEstimate(flops=2_000_000, bytes_accessed=moved, transcendentals=0),
    )(*args)


def per_device(field, phase_table, phase_ids):
    narrow_bits = lax.axis_size("narrow").bit_length() - 1
    level_count = phase_ids.shape[0]
    other_flip = 1 << 5 - narrow_bits
    table = phase_table.transpose(1, 2, 0, 3).reshape(RANK, RANK, RANK, RANK, 2, NTAB)
    f32 = jnp.float32
    state_shape = jax.ShapeDtypeStruct((POINTS, 2 * GATHERS, SLOTS), f32)
    tagged_shape = jax.ShapeDtypeStruct((POINTS + 1, 2 * GATHERS, SLOTS), f32)
    table_shape = jax.ShapeDtypeStruct((2, ROWS, NTAB), jnp.bfloat16)
    kern_shape = jax.ShapeDtypeStruct((ROWS, SLOTS), f32)
    state_scratch = pltpu.VMEM(state_shape.shape, f32)
    kern_scratch = pltpu.VMEM(kern_shape.shape, f32)
    bind = functools.partial

    def partner_of(state, *levels):
        if levels[0] < narrow_bits:
            return swapped(state, "narrow", list(levels))
        return swapped(state, "wide", [level - narrow_bits for level in levels])

    partner = partner_of(field, 0)
    ids_shape = jax.ShapeDtypeStruct((level_count, 2, 1, SLOTS), jnp.int32)
    weights = jnp.asarray(weight_tiles())
    hi, lo = call(
        table_kernel,
        (table_shape, table_shape),
        table,
        scratch=[
            pltpu.VMEM((2, RANK, RANK, RANK, 2, NTAB), f32),
            pltpu.VMEM((ROWS, NTAB), f32),
            pltpu.SemaphoreType.DMA((2 * RANK,)),
        ],
        space=HBM,
        limit=51 * MIB,
        moved=5 * MIB,
    )
    kern, acc, ids, other_ids = call(
        bind(first_kernel, other_flip),
        (kern_shape, state_shape, ids_shape, ids_shape),
        field,
        phase_ids,
        weights,
        hi,
        lo,
        scratch=[kern_scratch],
    )
    state, tagged = call(join_first, (state_shape, tagged_shape), acc, kern, partner, ids)

    near, both, far = partner_of(state, 1), partner_of(state, 1, 2), partner_of(tagged, 2)
    pairs = ((1, True), (2, True), (3, True), (4, True), (4, False), (5, True), (6, True))
    kerns = call(
        bind(later_kernels, pairs),
        jax.ShapeDtypeStruct((len(pairs), 2, ROWS, SLOTS), f32),
        ids,
        other_ids,
        weights,
        hi,
        lo,
    )
    acc = call(bind(half_kernel, 1, 0, 0), state_shape, state, kerns)
    kern, other = call(
        bind(other_first, 1), (kern_shape, state_shape), far, weights, hi, lo, scratch=[kern_scratch]
    )
    other = call(bind(far_kernel, 1, (), 1), state_shape, other, kern, both, kerns, scratch=[state_scratch])
    state = call(bind(near_kernel, 1, 0, 1), state_shape, acc, other, kerns, near, scratch=[state_scratch])

    partner = partner_of(state, 3)
    acc = call(bind(half_kernel, 1, 2, 0), state_shape, state, kerns)
    state = call(bind(join_kernel, 1, 2), state_shape, acc, kerns, partner)

    near, both, far = partner_of(state, 4), partner_of(state, 4, 5), partner_of(state, 5)
    acc = call(bind(half_kernel, 0, 3, 0), state_shape, state, kerns)
    other = call(bind(half_kernel, 0, 4, 0), state_shape, far, kerns)
    other = call(bind(far_kernel, 0, (4, 1), 5), state_shape, other, kerns, both, kerns, scratch=[state_scratch])
    state = call(bind(near_kernel, 0, 3, 5), state_shape, acc, other, kerns, near, scratch=[state_scratch])

    partner = partner_of(state, 6)
    acc = call(bind(half_kernel, 0, 6, 0), state_shape, state, kerns)
    return call(bind(join_kernel, 0, 6), jax.ShapeDtypeStruct(field.shape, f32), acc, kerns, partner)


def solution(mesh):
    in_specs = (P(None, None, None, ("wide", "narrow")), P(), P(None, None, "narrow", None))
    out_specs = P(None, None, None, ("wide", "narrow"))
    return jax.shard_map(
        per_device, mesh=mesh, in_specs=in_specs, out_specs=out_specs, check_vma=False
    )
```

```python
import functools

import jax
import jax.numpy as jnp
import numpy as np
from jax import lax
from jax.experimental import pallas as pl
from jax.experimental.pallas import tpu as pltpu
from jax.sharding import PartitionSpec as P

RANK = 5
POINTS = RANK * RANK
GATHERS = 4
SLOTS = 128
NTAB = 512
BLOCK = 64
ROWS = RANK * BLOCK

VMEM = pl.BlockSpec(memory_space=pltpu.VMEM)
HBM = pl.BlockSpec(memory_space=pltpu.HBM)
MIB = 1024 * 1024


def swapped(block, axis, bits):
    flip = sum(1 << bit for bit in bits)
    return lax.ppermute(block, axis, [(low, low ^ flip) for low in range(lax.axis_size(axis))])


def half_weights(order_count):
    cheb_nodes = 0.5 + 0.5 * np.cos(np.pi * (2 * np.arange(order_count) + 1) / (2 * order_count))
    result = np.zeros((2, order_count, order_count))
    for child_half in range(2):
        points = (cheb_nodes + child_half) / 2.0
        lagrange = np.ones((order_count, order_count))
        for column in range(order_count):
            for other_node in range(order_count):
                if other_node != column:
                    lagrange[:, column] *= (points - cheb_nodes[other_node]) / (
                        cheb_nodes[column] - cheb_nodes[other_node]
                    )
        result[child_half] = lagrange / np.sqrt(2.0 * np.mean(np.sum(lagrange * lagrange, axis=1)))
    return result


def weight_tiles():
    tiles = np.zeros((2, BLOCK, SLOTS), np.float32)
    tiles[:, : 2 * POINTS] = np.repeat(half_weights(RANK).reshape(2, POINTS, 1), 2, axis=1)
    return tiles


def point(parity, shared, moving):
    return moving * RANK + shared if parity == 0 else shared * RANK + moving


def level_bit(level):
    bits = lax.axis_size("narrow").bit_length() - 1
    if level < bits:
        return lax.axis_index("narrow") // 2**level % 2
    return lax.axis_index("wide") // 2 ** (level - bits) % 2


def turned(tile):
    return jnp.concatenate([-tile[GATHERS:], tile[:GATHERS]], axis=0)


def apply_side(parity, kern, source, start, finish):
    for shared in range(RANK):
        tiles = [source(point(parity, shared, v)) for v in range(RANK)]
        turns = [turned(t) for t in tiles]
        for u in range(RANK):
            total = start(point(parity, shared, u))
            for v in range(RANK):
                row = shared * BLOCK + 2 * (u * RANK + v)
                real = kern(row)
                imag = kern(row + 1)
                term = real * tiles[v] + imag * turns[v]
                total = term if total is None else total + term
            finish(point(parity, shared, u), total)


def gathered(first, second, bit, weights_ref, hi, lo):
    own = jnp.where(bit == 0, first, second)
    partner = jnp.where(bit == 0, second, first)
    entry = lax.broadcasted_iota(jnp.int32, (NTAB, SLOTS), 0)
    hot = jnp.concatenate(
        [jnp.where(entry == own, 1.0, 0.0), jnp.where(entry == partner, 1.0, 0.0)], axis=1
    ).astype(jnp.bfloat16)
    values = jnp.dot(hi, hot, preferred_element_type=jnp.float32) + jnp.dot(
        lo, hot, preferred_element_type=jnp.float32
    )
    weights = jnp.where(bit == 0, weights_ref[0], weights_ref[1])
    weights = jnp.concatenate([weights] * RANK, axis=0)
    return values[:, :SLOTS] * weights, values[:, SLOTS:] * weights


def kern_rows(ref, *lead):
    return lambda row: ref[lead + (pl.ds(row, 1), slice(None))]


def tiles_of(ref):
    if ref.shape[1] == POINTS:
        return lambda p: jnp.concatenate([ref[0, p], ref[1, p]], axis=0)
    return lambda p: ref[p]


def nothing(p):
    return None


def putter(ref):
    def put(p, tile):
        if ref.shape[1] == POINTS:
            ref[0, p] = tile[:GATHERS]
            ref[1, p] = tile[GATHERS:]
        else:
            ref[p] = tile

    return put


def table_kernel(table_hbm, hi_ref, lo_ref, table, flat, sems):
    copies = []
    for parity in range(2):
        for shared in range(RANK):
            if parity == 0:
                source = table_hbm.at[:, shared, :, shared]
            else:
                source = table_hbm.at[shared, :, shared, :]
            copies.append(pltpu.make_async_copy(source, table.at[parity, shared], sems.at[len(copies)]))
            copies[-1].start()
    for parity in range(2):
        for shared in range(RANK):
            tail = shared * BLOCK + 2 * POINTS
            flat[pl.ds(tail, BLOCK - 2 * POINTS)] = jnp.zeros((BLOCK - 2 * POINTS, NTAB), jnp.float32)
            copies[parity * RANK + shared].wait()
            for u in range(RANK):
                for v in range(RANK):
                    flat[pl.ds(shared * BLOCK + 2 * (u * RANK + v), 2)] = table[parity, shared, u, v]
        whole = flat[...]
        hi = whole.astype(jnp.bfloat16)
        hi_ref[parity] = hi
        lo_ref[parity] = (whole - hi.astype(jnp.float32)).astype(jnp.bfloat16)


def first_kernel(
    other_flip, field_ref, all_ids_ref, weights_ref, hi_ref, lo_ref,
    kern_ref, acc_ref, ids_ref, other_ref, next_ref, own,
):
    wide_index = lax.axis_index("wide")
    for device, ref in ((wide_index, ids_ref), (wide_index ^ other_flip, other_ref)):
        ref[...] = all_ids_ref[:, :, :, pl.ds(pl.multiple_of(device * SLOTS, SLOTS), SLOTS)]
    own[...], kern_ref[...] = gathered(
        ids_ref[0, 0], ids_ref[0, 1], level_bit(0), weights_ref, hi_ref[0], lo_ref[0]
    )
    apply_side(0, kern_rows(own), tiles_of(field_ref), nothing, putter(acc_ref))
    later_kernels(((1, True), (2, True)), ids_ref, other_ref, weights_ref, hi_ref, lo_ref, next_ref)


def later_kernels(pairs, ids_ref, other_ref, weights_ref, hi_ref, lo_ref, kern_ref):
    for at, (level, mine) in enumerate(pairs):
        ids = ids_ref if mine else other_ref
        parity = level % 2
        kern_ref[at, 0], kern_ref[at, 1] = gathered(
            ids[level, 0], ids[level, 1], level_bit(level), weights_ref, hi_ref[parity], lo_ref[parity]
        )


def join_first(acc_ref, kern_ref, field_ref, ids_ref, out_ref):
    apply_side(0, kern_rows(kern_ref), tiles_of(field_ref), tiles_of(acc_ref), putter(out_ref))
    out_ref[POINTS] = jnp.concatenate(
        [ids_ref[1, s].astype(jnp.float32) for s in range(2)] + [jnp.zeros((6, SLOTS), jnp.float32)], axis=0
    )


def half_kernel(parity, at, side, state_ref, kern_ref, acc_ref):
    apply_side(parity, kern_rows(kern_ref, at, side), tiles_of(state_ref), nothing, putter(acc_ref))


def join_kernel(parity, at, acc_ref, kern_ref, state_ref, out_ref):
    apply_side(parity, kern_rows(kern_ref, at, 1), tiles_of(state_ref), tiles_of(acc_ref), putter(out_ref))


def other_first(level, state_ref, weights_ref, hi_ref, lo_ref, kern_ref, acc_ref, own):
    parity = level % 2
    ids = state_ref[POINTS].astype(jnp.int32)
    own[...], kern_ref[...] = gathered(
        ids[0:1], ids[1:2], level_bit(level), weights_ref, hi_ref[parity], lo_ref[parity]
    )
    apply_side(parity, kern_rows(own), tiles_of(state_ref), nothing, putter(acc_ref))


def far_kernel(parity, kern_at, at, acc_ref, kern_ref, state_ref, kerns_ref, out_ref, mid):
    apply_side(parity, kern_rows(kern_ref, *kern_at), tiles_of(state_ref), tiles_of(acc_ref), putter(mid))
    apply_side(1 - parity, kern_rows(kerns_ref, at, 1), tiles_of(mid), nothing, putter(out_ref))


def near_kernel(parity, at, later, acc_ref, far_ref, kerns_ref, later_ref, state_ref, out_ref, mid):
    apply_side(parity, kern_rows(kerns_ref, at, 1), tiles_of(state_ref), tiles_of(acc_ref), putter(mid))
    apply_side(1 - parity, kern_rows(later_ref, later, 0), tiles_of(mid), tiles_of(far_ref), putter(out_ref))


def call(kernel, outs, *args, scratch=(), space=VMEM, limit=40 * MIB, moved=MIB):
    return pl.pallas_call(
        kernel,
        out_shape=outs,
        in_specs=[space] * len(args),
        out_specs=jax.tree.map(lambda _: VMEM, outs),
        scratch_shapes=scratch,
        compiler_params=pltpu.CompilerParams(vmem_limit_bytes=limit),
        cost_estimate=pl.CostEstimate(flops=2_000_000, bytes_accessed=moved, transcendentals=0),
    )(*args)


def per_device(field, phase_table, phase_ids):
    narrow_bits = lax.axis_size("narrow").bit_length() - 1
    level_count = phase_ids.shape[0]
    other_flip = 1 << 5 - narrow_bits
    table = phase_table.transpose(1, 2, 0, 3).reshape(RANK, RANK, RANK, RANK, 2, NTAB)
    f32 = jnp.float32
    state_shape = jax.ShapeDtypeStruct((POINTS, 2 * GATHERS, SLOTS), f32)
    tagged_shape = jax.ShapeDtypeStruct((POINTS + 1, 2 * GATHERS, SLOTS), f32)
    table_shape = jax.ShapeDtypeStruct((2, ROWS, NTAB), jnp.bfloat16)
    kern_shape = jax.ShapeDtypeStruct((ROWS, SLOTS), f32)
    state_scratch = pltpu.VMEM(state_shape.shape, f32)
    kern_scratch = pltpu.VMEM(kern_shape.shape, f32)
    bind = functools.partial

    def partner_of(state, *levels):
        if levels[0] < narrow_bits:
            return swapped(state, "narrow", list(levels))
        return swapped(state, "wide", [level - narrow_bits for level in levels])

    def kernels_of(*pairs):
        shape = jax.ShapeDtypeStruct((len(pairs), 2, ROWS, SLOTS), f32)
        return call(bind(later_kernels, pairs), shape, ids, other_ids, weights, hi, lo)

    partner = partner_of(field, 0)
    ids_shape = jax.ShapeDtypeStruct((level_count, 2, 1, SLOTS), jnp.int32)
    weights = jnp.asarray(weight_tiles())
    hi, lo = call(
        table_kernel,
        (table_shape, table_shape),
        table,
        scratch=[
            pltpu.VMEM((2, RANK, RANK, RANK, 2, NTAB), f32),
            pltpu.VMEM((ROWS, NTAB), f32),
            pltpu.SemaphoreType.DMA((2 * RANK,)),
        ],
        space=HBM,
        limit=51 * MIB,
        moved=5 * MIB,
    )
    kern, acc, ids, other_ids, kerns = call(
        bind(first_kernel, other_flip),
        (kern_shape, state_shape, ids_shape, ids_shape, jax.ShapeDtypeStruct((2, 2, ROWS, SLOTS), f32)),
        field,
        phase_ids,
        weights,
        hi,
        lo,
        scratch=[kern_scratch],
    )
    state = call(join_first, tagged_shape, acc, kern, partner, ids)

    near, both, far = partner_of(state, 1), partner_of(state, 1, 2), partner_of(state, 2)
    mid_kerns = kernels_of((3, True), (4, True), (4, False))
    acc = call(bind(half_kernel, 1, 0, 0), state_shape, state, kerns)
    kern, other = call(
        bind(other_first, 1), (kern_shape, state_shape), far, weights, hi, lo, scratch=[kern_scratch]
    )
    other = call(bind(far_kernel, 1, (), 1), state_shape, other, kern, both, kerns, scratch=[state_scratch])
    state = call(
        bind(near_kernel, 1, 0, 1), state_shape, acc, other, kerns, kerns, near, scratch=[state_scratch]
    )

    partner = partner_of(state, 3)
    acc = call(bind(half_kernel, 1, 0, 0), state_shape, state, mid_kerns)
    state = call(bind(join_kernel, 1, 0), state_shape, acc, mid_kerns, partner)

    near, both, far = partner_of(state, 4), partner_of(state, 4, 5), partner_of(state, 5)
    kerns = kernels_of((5, True), (6, True))
    acc = call(bind(half_kernel, 0, 1, 0), state_shape, state, mid_kerns)
    other = call(bind(half_kernel, 0, 2, 0), state_shape, far, mid_kerns)
    other = call(bind(far_kernel, 0, (2, 1), 0), state_shape, other, mid_kerns, both, kerns, scratch=[state_scratch])
    state = call(
        bind(near_kernel, 0, 1, 0), state_shape, acc, other, mid_kerns, kerns, near, scratch=[state_scratch]
    )

    partner = partner_of(state, 6)
    acc = call(bind(half_kernel, 0, 1, 0), state_shape, state, kerns)
    return call(bind(join_kernel, 0, 1), jax.ShapeDtypeStruct(field.shape, f32), acc, kerns, partner)


def solution(mesh):
    in_specs = (P(None, None, None, ("wide", "narrow")), P(), P(None, None, "narrow", None))
    out_specs = P(None, None, None, ("wide", "narrow"))
    return jax.shard_map(
        per_device, mesh=mesh, in_specs=in_specs, out_specs=out_specs, check_vma=False
    )
```
